128 devices in a mesh: dp: 2 (over y_hi), head: 8 (over z, y_lo), blk: 8 (over x, core).
Axes of the slice: x: 4, y: 4 (y_hi: 2, y_lo: 2; y = y_hi * 2 + y_lo), z: 4, core: 2. Of those that a mesh axis runs over, the one named last changes fastest.
Arguments:
- queries: bfloat16 [2048, 24576], P(('dp', 'blk', 'head')), may hold values from -60 to 60, as said below
- latent: bfloat16 [2048, 576], P(('dp', 'blk', 'head')), may hold values from -8 to 8
- key_up: bfloat16 [128, 512, 128], P('head'), may hold values from -0.25 to 0.25
- value_up: bfloat16 [128, 512, 128], P('head'), may hold values from -0.25 to 0.25
- out_grad: bfloat16 [2048, 16384], P(('dp', 'blk'), 'head'), may hold values from -6 to 6
- block_docs: int32 [2, 8], P('dp'), may hold values from 0 to 2, never falling along the last dimension, each value on 1 to 6 neighbouring positions
Outputs:
- attended: bfloat16 [2048, 16384], P(('dp', 'blk'), 'head')
- query_grad: bfloat16 [2048, 24576], P(('dp', 'blk'), 'head')
- latent_grad: float32 [2048, 576], P(('dp', 'blk', 'head'))
- key_up_grad: float32 [128, 512, 128], P('head')
- value_up_grad: float32 [128, 512, 128], P('head')
The draws below stay inside these ranges and needn't reach their ends.
Inputs may be any that keep to these rules, and one draw needn't show every extreme that they name: `queries`: query features, heads side by side. `block_docs`: document numbers never fall along a pack; each document covers 1 to 6 blocks, one exactly 6.
All inputs are finite; a program needn't handle non-finite values.
Results may differ from the reference program's by a relative error of at most 0.033.
Values may be sent and summed in bfloat16 or wider, within the bound.
No kernel may reach another device: no remote copies, remote signals or barrier semaphores. Data moves between devices by JAX's collectives and lax.ppermute only.
A program may use at most 192 MiB of HBM per device.

```python
import math
from functools import partial
import jax
import jax.numpy as jnp
import numpy as np
from jax import lax

NOPE = 128
ROPE = 64
LATENT = 512
VHEAD = 128
HEADS = 128
BLOCK = 128
PACK_TOK = 1024
PACK_BLOCKS = 8
DOCS = 3
DOC_MOST = 6
TOKENS = 2048
N_DP = 2


def draw_queries(key, part):
    key = jax.random.fold_in(key, 3)
    extent = (TOKENS, HEADS, NOPE + ROPE)
    values = jnp.clip(jax.random.normal(key, extent, jnp.float32), -5.0, 5.0)
    return values.reshape(TOKENS, HEADS * (NOPE + ROPE)).astype(jnp.bfloat16)


def draw_latent(key, part):
    key = jax.random.fold_in(key, 5)
    extent = (TOKENS, LATENT + ROPE)
    values = jnp.clip(jax.random.normal(key, extent, jnp.float32), -5.0, 5.0)
    return values.astype(jnp.bfloat16)


def level_of(stream_key, dims, pieces, least, top_value):
    def one(axis_at, blocks):
        heights = jax.random.uniform(jax.random.fold_in(jax.random.fold_in(stream_key, 6), axis_at), (blocks,), jnp.float32, least / len(pieces), top_value / len(pieces))
        return jnp.repeat(jnp.exp(heights), dims[axis_at] // blocks).reshape((-1,) + (1,) * (len(dims) - axis_at - 1))

    loudness = one(*pieces[0])
    for cut in pieces[1:]:
        loudness = loudness * one(*cut)
    return loudness


def length_profile(count, total, reach, lean):
    portions = [(1 << 20) // math.isqrt(standing ** lean) + 1 for standing in range(2, count + 1)]
    spare, counts = total - reach - (count - 1), [1] * (count - 1)
    while spare > 0:
        candidates = [i for i in range(count - 1) if counts[i] < reach]
        mass, remaining = sum([portions[i] for i in candidates]), spare
        for i in candidates:
            addition = min(reach - counts[i], max(1, remaining * portions[i] // mass), spare)
            counts[i] = counts[i] + addition
            spare = spare - addition
    return np.array([reach] + counts)


def uneven(own_key, number_of, total, bound, slope):
    if number_of == 2:
        one = jax.random.randint(own_key, (), max(1, total - bound), min(bound, total - 1) + 1)
        return jnp.stack([one, total - one])
    tallies = jnp.asarray(length_profile(number_of, total, bound, slope), jnp.int32)
    couples = (number_of - 1) // 2
    source_of, receiver = tallies[1:1 + 2 * couples:2], tallies[2:2 + 2 * couples:2]
    room = jnp.minimum(source_of - 1, bound - receiver)
    shifted = jax.random.randint(jax.random.fold_in(own_key, 1), (couples,), 0, 1 << 20) % (room + 1)
    tallies = tallies.at[1:1 + 2 * couples:2].set(source_of - shifted).at[2:2 + 2 * couples:2].set(receiver + shifted)
    return tallies[jax.random.permutation(jax.random.fold_in(own_key, 2), number_of)]


def gaussian(own_key, dims, deviation, limit, cuts=(), kind=jnp.bfloat16):
    drawn = jax.random.normal(own_key, dims, jnp.float32) * deviation
    if len(cuts) > 0:
        drawn = level_of(own_key, dims, cuts, -0.22, 0.18) * drawn
    return jnp.clip(drawn, min=-limit, max=limit).astype(kind)


def setup_inputs(seed: int = 0) -> dict:
    streams_of = jax.random.split(jax.random.key(seed), 7)
    queries = draw_queries(jax.random.fold_in(streams_of[6], 71), 0)
    latent = draw_latent(jax.random.fold_in(streams_of[6], 71), 0)
    key_up = gaussian(streams_of[2], (HEADS, LATENT, NOPE), LATENT ** -0.5, 0.25, ((0, 8),))
    value_up = gaussian(streams_of[3], (HEADS, LATENT, VHEAD), LATENT ** -0.5, 0.25, ((0, 8),))
    out_grad = gaussian(streams_of[4], (TOKENS, HEADS * VHEAD), 1.0, 6.0, ((0, 16), (1, 8)))
    block_docs = jax.vmap(lambda own: jnp.searchsorted(jnp.cumsum(uneven(own, DOCS, PACK_BLOCKS, DOC_MOST, 1)), jnp.arange(PACK_BLOCKS), side="right"))(jax.random.split(streams_of[5], N_DP)).reshape((N_DP, PACK_BLOCKS)).astype(jnp.int32)
    return {"queries": queries, "latent": latent, "key_up": key_up, "value_up": value_up, "out_grad": out_grad, "block_docs": block_docs}


def rounded(values):
    return lax.optimization_barrier(values.astype(jnp.bfloat16)).astype(jnp.float32)


def head_group(operands, keys_all, allowed):
    query_group, key_group, value_group, grad_group = operands
    score_scale = (NOPE + ROPE) ** -0.5
    query_nope = query_group[:, :, :NOPE].astype(jnp.float32)
    query_rotary = query_group[:, :, NOPE:].astype(jnp.float32)
    key_weights = key_group.astype(jnp.float32)
    value_weights = value_group.astype(jnp.float32)
    latent_nope = keys_all[:, :LATENT].astype(jnp.float32)
    latent_rotary = keys_all[:, LATENT:].astype(jnp.float32)
    query_lat = rounded(jnp.einsum('thn,hjn->thj', query_nope, key_weights))
    scores = (jnp.einsum('thj,kj->htk', query_lat, latent_nope)
              + jnp.einsum('thr,kr->htk', query_rotary, latent_rotary)) * score_scale
    masked = jnp.where(allowed[None], scores, jnp.float32(-1e30))
    row_top = jnp.max(masked, axis=-1)
    expo = jnp.where(allowed[None], jnp.exp(masked - row_top[..., None]), jnp.float32(0.0))
    row_total = jnp.sum(expo, axis=-1)
    weighted = jnp.einsum('htk,kj->thj', rounded(expo), latent_nope) / jnp.transpose(row_total)[..., None]
    context = rounded(weighted)
    attended = jnp.einsum('thj,hjv->thv', context, value_weights).astype(jnp.bfloat16)
    grad_values = grad_group.astype(jnp.float32)
    context_grad = rounded(jnp.einsum('thv,hjv->thj', grad_values, value_weights))
    value_grad = jnp.einsum('thj,thv->hjv', context, grad_values)
    delta = jnp.transpose(jnp.sum(context_grad * context, axis=-1))
    probs = expo / row_total[..., None]
    prob_grad = jnp.einsum('thj,kj->htk', context_grad, latent_nope)
    score_grad = rounded(probs * (prob_grad - delta[..., None]) * score_scale)
    lat_grad = rounded(jnp.einsum('htk,kj->thj', score_grad, latent_nope))
    rotary_grad = jnp.einsum('htk,kr->thr', score_grad, latent_rotary)
    nope_grad = jnp.einsum('thj,hjn->thn', lat_grad, key_weights)
    query_grad = jnp.concatenate([nope_grad, rotary_grad], axis=-1).astype(jnp.bfloat16)
    key_up_grad = jnp.einsum('thj,thn->hjn', lat_grad, query_nope)
    key_nope = (jnp.einsum('htk,thj->kj', score_grad, query_lat)
                + jnp.einsum('htk,thj->kj', rounded(probs), context_grad))
    key_rotary = jnp.einsum('htk,thr->kr', score_grad, query_rotary)
    latent_grad = jnp.concatenate([key_nope, key_rotary], axis=1)
    return attended, query_grad, key_up_grad, value_grad, latent_grad


def reference(queries, latent, key_up, value_up, out_grad, block_docs):
    query_dim = NOPE + ROPE
    group = math.gcd(HEADS, 8)
    groups = HEADS // group
    positions = jnp.arange(PACK_TOK, dtype=jnp.int32)
    attended_all, query_all, latent_all = [], [], []
    key_total = jnp.zeros((HEADS, LATENT, NOPE), jnp.float32)
    value_total = jnp.zeros((HEADS, LATENT, VHEAD), jnp.float32)
    key_groups = key_up.reshape(groups, group, LATENT, NOPE)
    value_groups = value_up.reshape(groups, group, LATENT, VHEAD)
    for pack_index in range(N_DP):
        first_row = pack_index * PACK_TOK
        keys_all = latent[first_row:first_row + PACK_TOK]
        token_docs = block_docs[pack_index][positions // BLOCK]
        allowed = (token_docs[None, :] == token_docs[:, None]) & (positions[None, :] <= positions[:, None])
        query_pack = queries[first_row:first_row + PACK_TOK].reshape(PACK_TOK, groups, group, query_dim)
        grad_pack = out_grad[first_row:first_row + PACK_TOK].reshape(PACK_TOK, groups, group, VHEAD)
        operands = (jnp.transpose(query_pack, (1, 0, 2, 3)), key_groups, value_groups,
                    jnp.transpose(grad_pack, (1, 0, 2, 3)))
        results = lax.map(partial(head_group, keys_all=keys_all, allowed=allowed), operands)
        attended_all.append(jnp.transpose(results[0], (1, 0, 2, 3)).reshape(PACK_TOK, HEADS * VHEAD))
        query_all.append(jnp.transpose(results[1], (1, 0, 2, 3)).reshape(PACK_TOK, HEADS * query_dim))
        key_total = key_total + results[2].reshape(HEADS, LATENT, NOPE)
        value_total = value_total + results[3].reshape(HEADS, LATENT, VHEAD)
        latent_all.append(jnp.sum(results[4], axis=0))
    return (jnp.concatenate(attended_all, axis=0), jnp.concatenate(query_all, axis=0),
            jnp.concatenate(latent_all, axis=0), key_total, value_total)
```

```python
import functools

import jax
import jax.numpy as jnp
from jax import lax
from jax.experimental import pallas as pl
from jax.experimental.pallas import tpu as pltpu
from jax.sharding import Mesh
from jax.sharding import PartitionSpec as P

NOPE = 128
ROPE = 64
LATENT = 512
VHEAD = 128
BLOCK = 128
QUERY = NOPE + ROPE
KEY = LATENT + ROPE
DOC_MOST = 6
WINDOW = DOC_MOST * BLOCK
PAIR = 2
ROWS = PAIR * BLOCK
SCALE = QUERY ** -0.5

bf16 = jnp.bfloat16
f32 = jnp.float32


def mul(a, b, dims=((1,), (0,))):
    return lax.dot_general(a, b, (dims, ((), ())), preferred_element_type=f32)


NT = ((1,), (1,))
TN = ((0,), (0,))


def attention_kernel(
    place, query_ref, own_ref, other_ref, key_ref, value_ref, grad_ref,
    attended_ref, query_grad_ref, kv_ref, keep_ref, send_ref,
    keys, flipped, bias, total,
):
    step = pl.program_id(0)
    core, first, doc_first, block = place[0], place[1], place[2], place[3]
    n_x = own_ref.shape[0]

    @pl.when(step == 0)
    def _():
        for x in range(n_x):
            keys[pl.ds(pl.multiple_of((2 * x + core) * BLOCK, BLOCK), BLOCK), :] = own_ref[x]
            keys[pl.ds(pl.multiple_of((2 * x + 1 - core) * BLOCK, BLOCK), BLOCK), :] = other_ref[x]
        window = keys[pl.ds(pl.multiple_of(first * BLOCK, BLOCK), WINDOW), :]
        flipped[:LATENT, :] = jnp.transpose(window[:, :LATENT])
        flipped[LATENT:, :] = jnp.transpose(window[:, LATENT:])
        key_at = first * BLOCK + lax.broadcasted_iota(jnp.int32, (WINDOW, ROWS), 0)
        query_at = block * BLOCK + lax.broadcasted_iota(jnp.int32, (WINDOW, ROWS), 1) % BLOCK
        seen = (key_at >= doc_first * BLOCK) & (key_at <= query_at)
        bias[...] = jnp.where(seen, f32(0.0), f32(-1e30))
        total[...] = jnp.zeros_like(total)

    window = keys.at[pl.ds(pl.multiple_of(first * BLOCK, BLOCK), WINDOW), :]
    latents = window[:, :LATENT]
    rotary = window[:, LATENT:]
    queries = query_ref[...].reshape(BLOCK, PAIR * QUERY)
    nope = [queries[:, e * QUERY:e * QUERY + NOPE] for e in range(PAIR)]
    turned = jnp.concatenate([queries[:, e * QUERY + NOPE:(e + 1) * QUERY] for e in range(PAIR)], axis=0)
    grads = [grad_ref[:, e * VHEAD:(e + 1) * VHEAD] for e in range(PAIR)]
    query_lat = jnp.concatenate([mul(key_ref[e], nope[e], NT) for e in range(PAIR)], axis=1).astype(bf16)
    context_grad = jnp.concatenate([mul(value_ref[e], grads[e], NT) for e in range(PAIR)], axis=1).astype(bf16)

    scores = (mul(latents, query_lat) + mul(rotary, turned, NT)) * SCALE + bias[...]
    top = jnp.max(scores, axis=0, keepdims=True)
    expo = jnp.exp(scores - top)
    inverse = 1.0 / jnp.sum(expo, axis=0, keepdims=True)
    context = (mul(flipped[:LATENT, :], expo.astype(bf16)) * inverse).astype(bf16)
    delta = jnp.sum(context.astype(f32) * context_grad.astype(f32), axis=0, keepdims=True)
    probs = expo * inverse
    score_grad = (probs * (mul(latents, context_grad) - delta) * SCALE).astype(bf16)
    low = probs.astype(bf16)
    lat_grad = mul(flipped[...], score_grad)
    turned_grad = lat_grad[LATENT:, :]
    lat_grad = lat_grad[:LATENT, :].astype(bf16)

    out = total.at[pl.ds(pl.multiple_of(first * BLOCK, BLOCK), WINDOW), :]
    out[:, :LATENT] += mul(score_grad, query_lat, NT) + mul(low, context_grad, NT)
    out[:, LATENT:] += mul(score_grad, turned)

    pieces = []
    for e in range(PAIR):
        at = slice(e * BLOCK, (e + 1) * BLOCK)
        attended_ref[:, e * VHEAD:(e + 1) * VHEAD] = mul(context[:, at], value_ref[e], TN).astype(bf16)
        pieces.append(mul(lat_grad[:, at], key_ref[e], TN))
        pieces.append(jnp.transpose(turned_grad[:, at]))
        kv_ref[e, :, :NOPE] = mul(lat_grad[:, at], nope[e]).astype(bf16)
        kv_ref[e, :, NOPE:] = mul(context[:, at], grads[e]).astype(bf16)
    query_grad_ref[...] = jnp.concatenate(pieces, axis=1).astype(bf16)

    @pl.when(step == pl.num_programs(0) - 1)
    def _():
        for x in range(n_x):
            keep_ref[x] = total[pl.ds(pl.multiple_of((2 * x + core) * BLOCK, BLOCK), BLOCK), :].astype(bf16)
            send_ref[x] = total[pl.ds(pl.multiple_of((2 * x + 1 - core) * BLOCK, BLOCK), BLOCK), :].astype(bf16)


def attention(place, arrived, own, other, key_up, value_up, out_grad):
    heads = key_up.shape[0]
    steps = heads // PAIR
    n_x = own.shape[0]
    tokens = 2 * n_x * BLOCK

    def turn(i, place):
        return lax.rem(i + (1 - place[0]) * (steps // 2), steps)

    whole = lambda shape: pl.BlockSpec(shape, lambda i, place: (0,) * len(shape))
    return pl.pallas_call(
        attention_kernel,
        grid_spec=pltpu.PrefetchScalarGridSpec(
            num_scalar_prefetch=1,
            grid=(steps,),
            in_specs=[
                pl.BlockSpec((BLOCK, PAIR * QUERY), lambda i, place: (0, turn(i, place))),
                whole(own.shape),
                whole(other.shape),
                pl.BlockSpec((PAIR, LATENT, NOPE), lambda i, place: (turn(i, place), 0, 0)),
                pl.BlockSpec((PAIR, LATENT, VHEAD), lambda i, place: (turn(i, place), 0, 0)),
                pl.BlockSpec((BLOCK, PAIR * VHEAD), lambda i, place: (0, turn(i, place))),
            ],
            out_specs=[
                pl.BlockSpec((BLOCK, PAIR * VHEAD), lambda i, place: (0, turn(i, place))),
                pl.BlockSpec((BLOCK, PAIR * QUERY), lambda i, place: (0, turn(i, place))),
                pl.BlockSpec((PAIR, LATENT, NOPE + VHEAD), lambda i, place: (i, 0, 0)),
                whole(own.shape),
                whole(own.shape),
            ],
            scratch_shapes=[
                pltpu.VMEM((tokens, KEY), bf16),
                pltpu.VMEM((KEY, WINDOW), bf16),
                pltpu.VMEM((WINDOW, ROWS), f32),
                pltpu.VMEM((tokens, KEY), f32),
            ],
        ),
        out_shape=[
            jax.ShapeDtypeStruct((BLOCK, heads * VHEAD), bf16),
            jax.ShapeDtypeStruct((BLOCK, heads * QUERY), bf16),
            jax.ShapeDtypeStruct((heads, LATENT, NOPE + VHEAD), bf16),
            jax.ShapeDtypeStruct(own.shape, bf16),
            jax.ShapeDtypeStruct(own.shape, bf16),
        ],
        compiler_params=pltpu.CompilerParams(
            dimension_semantics=("arbitrary",), vmem_limit_bytes=48 * 1024 * 1024
        ),
        cost_estimate=pl.CostEstimate(
            flops=12_000_000_000, bytes_accessed=15_000_000, transcendentals=2_000_000
        ),
    )(place, arrived, own, other, key_up, value_up, out_grad)


def swapped(value):
    return lax.ppermute(value, "core", [(0, 1), (1, 0)])


def spread(value, axes):
    count = lax.axis_size(axes)
    return lax.all_to_all(
        jnp.broadcast_to(value[None], (count,) + value.shape), axes, 0, 0, tiled=True
    )


def on_device(queries, latent, key_up, value_up, out_grad, block_docs):
    heads = key_up.shape[0]
    n_head = lax.axis_size(("z", "y"))
    n_x = lax.axis_size("x")
    core = lax.axis_index("core")
    block = lax.axis_index("x") * 2 + core
    docs = block_docs[0]
    doc_first = jnp.sum((docs < docs[block]).astype(jnp.int32))
    first = jnp.maximum(block - (DOC_MOST - 1), 0)
    place = jnp.stack([core, first, doc_first, block]).astype(jnp.int32)

    rows = queries.shape[0]
    packed = jnp.concatenate(
        [
            queries.reshape(rows, n_head, heads * QUERY),
            jnp.broadcast_to(latent[:, None, :], (rows, n_head, KEY)),
        ],
        axis=2,
    )
    arrived = lax.all_to_all(packed, ("z", "y"), split_axis=1, concat_axis=0, tiled=False)
    arrived = arrived.reshape(rows * n_head, heads * QUERY + KEY)
    own = spread(arrived[:, heads * QUERY:], "x")
    other = swapped(own)

    attended, query_grad, kv, keep, send = attention(
        place, arrived, own, other, key_up, value_up, out_grad
    )

    half = heads // 2
    kv = (kv[half:].astype(f32) + swapped(kv[:half]).astype(f32)).astype(bf16)
    keep = (keep.astype(f32) + swapped(send).astype(f32)).astype(bf16)
    keep = lax.all_to_all(
        keep.reshape(n_x * n_head, rows, KEY), ("x", "z", "y"), 0, 0, tiled=True
    )
    latent_grad = jnp.sum(keep.astype(f32), axis=0)
    kv = lax.all_to_all(kv, ("dp", "x"), 0, 0, tiled=True)
    kv = jnp.sum(kv.astype(f32), axis=0).astype(bf16)
    mine = spread(kv, ("dp", "x"))
    others = swapped(mine)
    low = jnp.where(core == 0, mine, others)
    high = jnp.where(core == 0, others, mine)
    kv = jnp.concatenate([low, high], axis=0).astype(f32)
    return (attended, query_grad, latent_grad, kv[:, :, :NOPE], kv[:, :, NOPE:])


def solution(mesh):
    n_dp, n_head, n_blk = mesh.devices.shape
    fine = Mesh(
        mesh.devices.reshape(n_dp, n_head // 2, 2, n_blk // 2, 2), ("dp", "z", "y", "x", "core")
    )
    head, blk = ("z", "y"), ("x", "core")
    return jax.shard_map(
        on_device,
        mesh=fine,
        in_specs=(
            P(("dp",) + blk + head, None),
            P(("dp",) + blk + head, None),
            P(head, None, None),
            P(head, None, None),
            P(("dp",) + blk, head),
            P("dp", None),
        ),
        out_specs=(
            P(("dp",) + blk, head),
            P(("dp",) + blk, head),
            P(("dp",) + blk + head, None),
            P(head, None, None),
            P(head, None, None),
        ),
        check_vma=False,
    )
```

```python
import jax
import jax.numpy as jnp
from jax import lax
from jax.experimental import pallas as pl
from jax.experimental.pallas import tpu as pltpu
from jax.sharding import Mesh
from jax.sharding import PartitionSpec as P

NOPE = 128
ROPE = 64
LATENT = 512
VHEAD = 128
BLOCK = 128
QUERY = NOPE + ROPE
KEY = LATENT + ROPE
KEY_PAD = 640
DOC_MOST = 6
WINDOW = DOC_MOST * BLOCK
GROUP = 4
ROWS = GROUP * BLOCK
HALF = LATENT // 2
SCALE = QUERY ** -0.5
MIB = 1024 * 1024

bf16 = jnp.bfloat16
f32 = jnp.float32
NT = ((1,), (1,))
TN = ((0,), (0,))
HEAD_AXES = ("z", "y")
SUM_AXES = ("dp", "x")


def mul(a, b, dims=((1,), (0,))):
    return lax.dot_general(a, b, (dims, ((), ())), preferred_element_type=f32)


def at_block(block):
    return pl.ds(pl.multiple_of(block * BLOCK, BLOCK), BLOCK)


def attention_kernel(
    place, query_ref, own_ref, other_ref, key_ref, value_ref, grad_ref,
    attended_ref, query_grad_ref, kv_keep_ref, kv_send_ref, keep_ref, send_ref,
    keys, flipped, bias, total,
):
    step = pl.program_id(0)
    core, first, doc_first, x_here = place[0], place[1], place[2], place[3]
    z_here, y_here = place[4], place[5]
    n_x = own_ref.shape[0]
    block = x_here * 2 + core

    @pl.when(step == 0)
    def _():
        for s in range(n_x):
            x = lax.rem(x_here + n_x - s, n_x)
            keys[at_block(2 * x + core), :] = own_ref[s]
            keys[at_block(2 * x + 1 - core), :] = other_ref[s]
        window = keys[pl.ds(pl.multiple_of(first * BLOCK, BLOCK), WINDOW), :]
        flipped[:LATENT, :] = jnp.transpose(window[:, :LATENT])
        flipped[LATENT:, :] = jnp.transpose(window[:, LATENT:])
        key_at = first * BLOCK + lax.broadcasted_iota(jnp.int32, (WINDOW, BLOCK), 0)
        query_at = block * BLOCK + lax.broadcasted_iota(jnp.int32, (WINDOW, BLOCK), 1)
        seen = (key_at >= doc_first * BLOCK) & (key_at <= query_at)
        bias[...] = jnp.where(seen, f32(0.0), f32(-1e30))
        total[...] = jnp.zeros_like(total)

    window = keys.at[pl.ds(pl.multiple_of(first * BLOCK, BLOCK), WINDOW), :]
    latents = window[:, :LATENT]
    rotary = window[:, LATENT:]
    queries = query_ref[...]
    nope = [queries[:, e * QUERY:e * QUERY + NOPE] for e in range(GROUP)]
    turned = jnp.concatenate(
        [queries[:, e * QUERY + NOPE:(e + 1) * QUERY] for e in range(GROUP)], axis=0
    )
    grads = [grad_ref[:, e * VHEAD:(e + 1) * VHEAD] for e in range(GROUP)]
    query_lat = jnp.concatenate(
        [mul(key_ref[e], nope[e], NT).astype(bf16) for e in range(GROUP)], axis=1
    )
    context_grad = jnp.concatenate(
        [mul(value_ref[e], grads[e], NT).astype(bf16) for e in range(GROUP)], axis=1
    )

    hidden = jnp.concatenate([bias[...]] * GROUP, axis=1)
    scores = (mul(latents, query_lat) + mul(rotary, turned, NT)) * SCALE + hidden
    top = jnp.max(scores, axis=0, keepdims=True)
    expo = jnp.exp(scores - top)
    inverse = 1.0 / jnp.sum(expo, axis=0, keepdims=True)
    context = (mul(flipped[:LATENT, :], expo.astype(bf16)) * inverse).astype(bf16)
    delta = jnp.sum(context.astype(f32) * context_grad.astype(f32), axis=0, keepdims=True)
    probs = expo * inverse
    score_grad = (probs * (mul(latents, context_grad) - delta) * SCALE).astype(bf16)
    low = probs.astype(bf16)
    lat_grad = mul(flipped[...], score_grad)
    turned_grad = lat_grad[LATENT:, :]
    lat_grad = lat_grad[:LATENT, :].astype(bf16)

    out = total.at[pl.ds(pl.multiple_of(first * BLOCK, BLOCK), WINDOW), :]
    out[:, :LATENT] += mul(score_grad, query_lat, NT) + mul(low, context_grad, NT)
    out[:, LATENT:] += mul(score_grad, turned)

    pieces = []
    for e in range(GROUP):
        at = slice(e * BLOCK, (e + 1) * BLOCK)
        attended_ref[:, e * VHEAD:(e + 1) * VHEAD] = mul(context[:, at], value_ref[e], TN).astype(bf16)
        pieces.append(mul(lat_grad[:, at], key_ref[e], TN))
        pieces.append(jnp.transpose(turned_grad[:, at]))
        pair = jnp.concatenate([mul(lat_grad[:, at], nope[e]), mul(context[:, at], grads[e])], axis=1)
        upper, lower = pair[:HALF], pair[HALF:]
        kv_keep_ref[e] = jnp.where(core == 0, upper, lower).astype(bf16)
        kv_send_ref[e] = jnp.where(core == 0, lower, upper).astype(bf16)
    query_grad_ref[...] = jnp.concatenate(pieces, axis=1).astype(bf16)

    @pl.when(step == pl.num_programs(0) - 1)
    def _():
        n_z, n_y, _, rows = keep_ref.shape[:4]
        empty = jnp.zeros((rows, KEY_PAD - KEY), bf16)
        for dz in range(n_z):
            for dy in range(n_y):
                head = lax.rem(z_here + dz, n_z) * n_y + lax.rem(y_here + dy, n_y)
                for dx in range(n_x):
                    x = lax.rem(x_here + dx, n_x)
                    for ref, parity in ((keep_ref, core), (send_ref, 1 - core)):
                        start = pl.multiple_of((2 * x + parity) * BLOCK + head * rows, rows)
                        ref[dz, dy, dx, :, :KEY] = total[pl.ds(start, rows), :].astype(bf16)
                        ref[dz, dy, dx, :, KEY:] = empty


def attention(place, queries, own, other, key_up, value_up, out_grad, n_z, n_y):
    heads = key_up.shape[0]
    n_x = own.shape[0]
    tokens = 2 * n_x * BLOCK
    whole = lambda shape: pl.BlockSpec(shape, lambda i, place: (0,) * len(shape))
    heads_at = lambda i, place: (i, 0, 0)
    lanes_at = lambda i, place: (0, i)
    kv_spec = pl.BlockSpec((GROUP, HALF, NOPE + VHEAD), heads_at)
    kv_shape = jax.ShapeDtypeStruct((heads, HALF, NOPE + VHEAD), bf16)
    rows_shape = jax.ShapeDtypeStruct((n_z, n_y, n_x, BLOCK // (n_z * n_y), KEY_PAD), bf16)
    return pl.pallas_call(
        attention_kernel,
        grid_spec=pltpu.PrefetchScalarGridSpec(
            num_scalar_prefetch=1,
            grid=(heads // GROUP,),
            in_specs=[
                pl.BlockSpec((BLOCK, GROUP * QUERY), lanes_at),
                whole(own.shape),
                whole(other.shape),
                pl.BlockSpec((GROUP, LATENT, NOPE), heads_at),
                pl.BlockSpec((GROUP, LATENT, VHEAD), heads_at),
                pl.BlockSpec((BLOCK, GROUP * VHEAD), lanes_at),
            ],
            out_specs=[
                pl.BlockSpec((BLOCK, GROUP * VHEAD), lanes_at),
                pl.BlockSpec((BLOCK, GROUP * QUERY), lanes_at),
                kv_spec,
                kv_spec,
                whole(rows_shape.shape),
                whole(rows_shape.shape),
            ],
            scratch_shapes=[
                pltpu.VMEM((tokens, KEY), bf16),
                pltpu.VMEM((KEY, WINDOW), bf16),
                pltpu.VMEM((WINDOW, BLOCK), f32),
                pltpu.VMEM((tokens, KEY), f32),
            ],
        ),
        out_shape=[
            jax.ShapeDtypeStruct((BLOCK, heads * VHEAD), bf16),
            jax.ShapeDtypeStruct((BLOCK, heads * QUERY), bf16),
            kv_shape,
            kv_shape,
            rows_shape,
            rows_shape,
        ],
        name="attention",
        compiler_params=pltpu.CompilerParams(
            dimension_semantics=("arbitrary",), vmem_limit_bytes=48 * MIB
        ),
        cost_estimate=pl.CostEstimate(
            flops=12_000_000_000, bytes_accessed=15_000_000, transcendentals=1_600_000
        ),
    )(place, queries, own, other, key_up, value_up, out_grad)


def unfold(place, rows, begun, which):
    heads = rows.shape[0]
    each = heads // 2
    shape = jax.ShapeDtypeStruct((heads, LATENT, NOPE), f32)

    def kernel(place, rows_ref, *refs):
        key_ref, value_ref = refs[-2:]
        key_ref[...] = rows_ref[:, :, :NOPE].astype(f32)
        value_ref[...] = rows_ref[:, :, NOPE:].astype(f32)

    def half_at(i, place):
        return (i, place[0] if which == 0 else 1 - place[0], 0)

    out_spec = pl.BlockSpec((each, HALF, NOPE), half_at)
    return pl.pallas_call(
        kernel,
        grid_spec=pltpu.PrefetchScalarGridSpec(
            num_scalar_prefetch=1,
            grid=(heads // each,),
            in_specs=[pl.BlockSpec((each, HALF, NOPE + VHEAD), lambda i, place: (i, 0, 0))]
            + [pl.BlockSpec(memory_space=pl.ANY)] * len(begun),
            out_specs=[out_spec, out_spec],
        ),
        out_shape=[shape, shape],
        input_output_aliases={2: 0, 3: 1} if begun else {},
        name=f"unfold_{which}",
        cost_estimate=pl.CostEstimate(flops=0, bytes_accessed=6_000_000, transcendentals=0),
    )(place, rows, *begun)


def swapped(value):
    return lax.ppermute(value, "core", [(0, 1), (1, 0)])


def shifted(value, axis, steps):
    count = lax.axis_size(axis)
    return lax.ppermute(value, axis, [(i, (i + steps) % count) for i in range(count)])


def exchanged(value, axes):
    return lax.all_to_all(value, axes, 0, 0, tiled=True)


def copies(value, count):
    return jnp.broadcast_to(value[None], (count,) + value.shape)


def added(*terms):
    return sum(term.astype(f32) for term in terms)


def folded(rows, axis):
    count = rows.shape[0]
    return added(rows[0], *[shifted(rows[s], axis, s) for s in range(1, count)])


def on_device(queries, latent, key_up, value_up, out_grad, block_docs):
    n_head = lax.axis_size(HEAD_AXES)
    n_x = lax.axis_size("x")
    n_sum = lax.axis_size(SUM_AXES)
    core = lax.axis_index("core")
    x_here = lax.axis_index("x")
    block = x_here * 2 + core
    n_z, n_y = [lax.axis_size(axis) for axis in HEAD_AXES]
    docs = block_docs[0]
    doc_first = jnp.sum((docs < docs[block]).astype(jnp.int32))
    first = jnp.maximum(block - (DOC_MOST - 1), 0)
    place = jnp.stack(
        [core, first, doc_first, x_here] + [lax.axis_index(axis) for axis in HEAD_AXES]
    ).astype(jnp.int32)

    rows = queries.shape[0]
    arrived = jnp.swapaxes(queries.reshape(rows, n_head, -1), 0, 1)
    own = exchanged(copies(latent, n_head), HEAD_AXES)
    own, arrived = lax.optimization_barrier((own, arrived))
    arrived = exchanged(arrived, HEAD_AXES).reshape(rows * n_head, -1)
    own = own.reshape(BLOCK, KEY)
    own = jnp.stack([own] + [shifted(own, "x", s) for s in range(1, n_x)])
    other = swapped(own)

    attended, query_grad, keep, send, rows_keep, rows_send = attention(
        place, arrived, own, other, key_up, value_up, out_grad, n_z, n_y
    )
    kv = exchanged(added(keep, swapped(send)).astype(bf16), SUM_AXES)
    rows = added(rows_keep, swapped(rows_send)).astype(bf16)
    for axis in HEAD_AXES:
        rows = folded(rows, axis).astype(bf16)
    kv = added(*kv.reshape((n_sum, -1) + kv.shape[1:])).astype(bf16)
    kv, rows = lax.optimization_barrier((kv, rows))
    rows = [rows[0]] + [shifted(rows[s], "x", s) for s in range(1, n_x)]
    kv = exchanged(copies(kv, n_sum), SUM_AXES).reshape((-1,) + kv.shape[1:])
    grads = unfold(place, kv, [], 0)
    grads = unfold(place, swapped(kv), grads, 1)
    rows, grads = lax.optimization_barrier((rows, grads))
    latent_grad = added(*rows)[:, :KEY]
    key_up_grad, value_up_grad = grads
    return (attended, query_grad, latent_grad, key_up_grad, value_up_grad)


def solution(mesh):
    n_dp, n_head, n_blk = mesh.devices.shape
    fine = Mesh(
        mesh.devices.reshape(n_dp, n_head // 2, 2, n_blk // 2, 2), ("dp", "z", "y", "x", "core")
    )
    head, blk = HEAD_AXES, ("x", "core")
    return jax.shard_map(
        on_device,
        mesh=fine,
        in_specs=(
            P(("dp",) + blk + head, None),
            P(("dp",) + blk + head, None),
            P(head, None, None),
            P(head, None, None),
            P(("dp",) + blk, head),
            P("dp", None),
        ),
        out_specs=(
            P(("dp",) + blk, head),
            P(("dp",) + blk, head),
            P(("dp",) + blk + head, None),
            P(head, None, None),
            P(head, None, None),
        ),
        check_vma=False,
    )
```

```python
import jax
import jax.numpy as jnp
from jax import lax
from jax.experimental import pallas as pl
from jax.experimental.pallas import tpu as pltpu
from jax.sharding import Mesh
from jax.sharding import PartitionSpec as P

NOPE = 128
ROPE = 64
LATENT = 512
VHEAD = 128
BLOCK = 128
QUERY = NOPE + ROPE
KEY = LATENT + ROPE
KEY_PAD = 640
HALF = LATENT // 2
DOC_MOST = 6
WINDOW = DOC_MOST * BLOCK
GROUP = 4
ROWS = GROUP * BLOCK
SCALE = QUERY ** -0.5
MIB = 1024 * 1024

bf16 = jnp.bfloat16
f32 = jnp.float32
NT = ((1,), (1,))
TN = ((0,), (0,))
HEAD_AXES = ("z", "y")


def mul(a, b, dims=((1,), (0,))):
    return lax.dot_general(a, b, (dims, ((), ())), preferred_element_type=f32)


def at_block(block):
    return pl.ds(pl.multiple_of(block * BLOCK, BLOCK), BLOCK)


def attention_kernel(
    place, query_ref, own_ref, other_ref, key_ref, value_ref, grad_ref, got_grad_ref,
    attended_ref, query_grad_ref, far_right_ref, far_left_ref, right_top_ref, right_low_ref,
    left_top_ref, left_low_ref, stay_ref, keep_ref, send_ref,
    keys, flipped, bias, total,
):
    group = pl.program_id(0)
    core, x_here, z_here, y_here = place[0], place[1], place[2], place[3]
    n_x = own_ref.shape[0]
    sides = range(2)
    firsts = [jnp.maximum(x_here * 2 + side - (DOC_MOST - 1), 0) for side in sides]

    @pl.when(group == 0)
    def _():
        for s in range(n_x):
            x = lax.rem(x_here + n_x - s, n_x)
            keys[at_block(2 * x + core), :] = own_ref[s]
            keys[at_block(2 * x + 1 - core), :] = other_ref[s]
        flipped[:LATENT, :] = jnp.transpose(keys[:, :LATENT])
        flipped[LATENT:, :] = jnp.transpose(keys[:, LATENT:])
        total[...] = jnp.zeros_like(total)
        for side in sides:
            key_at = firsts[side] * BLOCK + lax.broadcasted_iota(jnp.int32, (WINDOW, BLOCK), 0)
            query_at = (x_here * 2 + side) * BLOCK + lax.broadcasted_iota(jnp.int32, (WINDOW, BLOCK), 1)
            seen = (key_at >= place[4 + side] * BLOCK) & (key_at <= query_at)
            bias[side] = jnp.where(seen, f32(0.0), f32(-1e30))

    here = [pl.ds(pl.multiple_of(first * BLOCK, BLOCK), WINDOW) for first in firsts]
    window = [keys.at[here[side], :] for side in sides]
    heads = range(GROUP)
    at = [slice(e * BLOCK, (e + 1) * BLOCK) for e in heads]
    queries = [query_ref[side] for side in sides]
    nope = [[queries[side][:, e * QUERY:e * QUERY + NOPE] for e in heads] for side in sides]
    turned = [
        jnp.concatenate([queries[side][:, e * QUERY + NOPE:(e + 1) * QUERY] for e in heads], axis=0)
        for side in sides
    ]
    all_grads = [jnp.where(side == core, grad_ref[...], got_grad_ref[...]) for side in sides]
    grads = [[all_grads[side][:, e * VHEAD:(e + 1) * VHEAD] for e in heads] for side in sides]
    query_lat = [
        jnp.concatenate([mul(key_ref[e], nope[side][e], NT).astype(bf16) for e in heads], axis=1)
        for side in sides
    ]
    context_grad = [
        jnp.concatenate([mul(value_ref[e], grads[side][e], NT).astype(bf16) for e in heads], axis=1)
        for side in sides
    ]

    def scores_of(side):
        hidden = jnp.concatenate([bias[side]] * GROUP, axis=1)
        latents, rotary = window[side][:, :LATENT], window[side][:, LATENT:]
        return (mul(latents, query_lat[side]) + mul(rotary, turned[side], NT)) * SCALE + hidden

    def softmax_of(scores):
        top = jnp.max(scores, axis=0, keepdims=True)
        expo = jnp.exp(scores - top)
        return expo, 1.0 / jnp.sum(expo, axis=0, keepdims=True)

    def context_of(side, expo, inverse):
        context = (mul(flipped[:LATENT, here[side]], expo.astype(bf16)) * inverse).astype(bf16)
        delta = jnp.sum(
            context.astype(f32) * context_grad[side].astype(f32), axis=0, keepdims=True
        )
        return context, delta

    def score_grad_of(side, expo, inverse, delta):
        probs = expo * inverse
        grad = mul(window[side][:, :LATENT], context_grad[side]) - delta
        return (probs * grad * SCALE).astype(bf16), probs.astype(bf16)

    def lat_grad_of(side, score_grad, low):
        lat_grad = mul(flipped[:, here[side]], score_grad)
        out = total.at[here[side], :]
        out[:, :LATENT] += mul(score_grad, query_lat[side], NT) + mul(low, context_grad[side], NT)
        out[:, LATENT:] += mul(score_grad, turned[side])
        return lat_grad[:LATENT, :].astype(bf16), lat_grad[LATENT:, :]

    scores = [scores_of(side) for side in sides]
    soft = [softmax_of(scores[side]) for side in sides]
    contexts = [context_of(side, *soft[side]) for side in sides]
    score_grads = [score_grad_of(side, *soft[side], contexts[side][1]) for side in sides]
    lat_grads = [lat_grad_of(side, *score_grads[side]) for side in sides]

    for side in sides:
        slot = lax.rem(side + core, 2)
        pieces = []
        for e in heads:
            pieces.append(mul(lat_grads[side][0][:, at[e]], key_ref[e], TN))
            pieces.append(jnp.transpose(lat_grads[side][1][:, at[e]]))
            attended_ref[slot, :, e * VHEAD:(e + 1) * VHEAD] = mul(
                contexts[side][0][:, at[e]], value_ref[e], TN
            ).astype(bf16)
        query_grad_ref[slot] = jnp.concatenate(pieces, axis=1).astype(bf16)
    both = lambda parts, axis: jnp.concatenate(parts, axis=axis)
    for e in heads:
        grad = both(
            [
                mul(both([side[0][:, at[e]] for side in lat_grads], 1), both([side[e] for side in nope], 0)),
                mul(both([side[0][:, at[e]] for side in contexts], 1), both([side[e] for side in grads], 0)),
            ],
            1,
        ).astype(bf16)
        top, low = grad[:HALF], grad[HALF:]
        away = lax.rem(e - x_here + n_x, n_x)
        places = (
            ((stay_ref, slice(0, HALF), top), (stay_ref, slice(HALF, LATENT), low)),
            ((right_top_ref, slice(0, HALF), top), (right_low_ref, slice(0, HALF), low)),
            ((far_right_ref, slice(0, HALF), top), (far_left_ref, slice(0, HALF), low)),
            ((left_top_ref, slice(0, HALF), top), (left_low_ref, slice(0, HALF), low)),
        )
        for distance, writes in enumerate(places):

            @pl.when(away == distance)
            def _():
                for ref, where, value in writes:
                    ref[0, where, :] = value

    @pl.when(group == pl.num_programs(0) - 1)
    def _():
        n_z, n_y, _, rows = keep_ref.shape[:4]
        empty = jnp.zeros((rows, KEY_PAD - KEY), bf16)
        for dz in range(n_z):
            for dy in range(n_y):
                head = lax.rem(z_here + dz, n_z) * n_y + lax.rem(y_here + dy, n_y)
                for dx in range(n_x):
                    x = lax.rem(x_here + dx, n_x)
                    for ref, parity in ((keep_ref, core), (send_ref, 1 - core)):
                        start = pl.multiple_of((2 * x + parity) * BLOCK + head * rows, rows)
                        ref[dz, dy, dx, :, :KEY] = total[pl.ds(start, rows), :].astype(bf16)
                        ref[dz, dy, dx, :, KEY:] = empty


def attention(place, queries, own, other, key_up, value_up, out_grad, got_grad, n_z, n_y):
    heads = key_up.shape[0] // 2
    groups = heads // GROUP
    n_x = own.shape[0]
    tokens = 2 * n_x * BLOCK
    whole = lambda shape: pl.BlockSpec(shape, lambda g, place: (0,) * len(shape))
    weights_at = lambda g, place: (place[0] * groups + g, 0, 0)
    sides_at = lambda g, place: (0, 0, g)
    side_at = lambda g, place: (g, 0, 0)
    rows_shape = jax.ShapeDtypeStruct((n_z, n_y, n_x, BLOCK // (n_z * n_y), KEY_PAD), bf16)
    return pl.pallas_call(
        attention_kernel,
        grid_spec=pltpu.PrefetchScalarGridSpec(
            num_scalar_prefetch=1,
            grid=(groups,),
            in_specs=[
                pl.BlockSpec((2, BLOCK, GROUP * QUERY), sides_at),
                whole(own.shape),
                whole(other.shape),
                pl.BlockSpec((GROUP, LATENT, NOPE), weights_at),
                pl.BlockSpec((GROUP, LATENT, VHEAD), weights_at),
                pl.BlockSpec((BLOCK, GROUP * VHEAD), lambda g, place: (0, place[0] * groups + g)),
                pl.BlockSpec((BLOCK, GROUP * VHEAD), lambda g, place: (0, g)),
            ],
            out_specs=[
                pl.BlockSpec((2, BLOCK, GROUP * VHEAD), sides_at),
                pl.BlockSpec((2, BLOCK, GROUP * QUERY), sides_at),
                *[pl.BlockSpec((1, HALF, NOPE + VHEAD), side_at)] * 6,
                pl.BlockSpec((1, LATENT, NOPE + VHEAD), side_at),
                whole(rows_shape.shape),
                whole(rows_shape.shape),
            ],
            scratch_shapes=[
                pltpu.VMEM((tokens, KEY), bf16),
                pltpu.VMEM((KEY, tokens), bf16),
                pltpu.VMEM((2, WINDOW, BLOCK), f32),
                pltpu.VMEM((tokens, KEY), f32),
            ],
        ),
        out_shape=[
            jax.ShapeDtypeStruct((2, BLOCK, heads * VHEAD), bf16),
            jax.ShapeDtypeStruct((2, BLOCK, heads * QUERY), bf16),
            *[jax.ShapeDtypeStruct((groups, HALF, NOPE + VHEAD), bf16)] * 6,
            jax.ShapeDtypeStruct((groups, LATENT, NOPE + VHEAD), bf16),
            rows_shape,
            rows_shape,
        ],
        name="attention",
        compiler_params=pltpu.CompilerParams(
            dimension_semantics=("arbitrary",), vmem_limit_bytes=48 * MIB
        ),
        cost_estimate=pl.CostEstimate(
            flops=12_000_000_000, bytes_accessed=15_000_000, transcendentals=1_600_000
        ),
    )(place, queries, own, other, key_up, value_up, out_grad, got_grad)


def join(place, *pairs):
    def kernel(place, *refs):
        count = len(pairs)
        for n in range(count):
            mine_ref, got_ref, out_ref = refs[2 * n], refs[2 * n + 1], refs[2 * count + n]
            width = mine_ref.shape[1]
            for ref, core in ((mine_ref, place[0]), (got_ref, 1 - place[0])):
                out_ref[:, pl.ds(pl.multiple_of(core * width, 128), width)] = ref[...]

    whole = lambda shape: pl.BlockSpec(shape, lambda i, place: (0,) * len(shape))
    shapes = [(mine.shape[0], 2 * mine.shape[1]) for mine, _ in pairs]
    return pl.pallas_call(
        kernel,
        grid_spec=pltpu.PrefetchScalarGridSpec(
            num_scalar_prefetch=1,
            grid=(1,),
            in_specs=[whole(value.shape) for pair in pairs for value in pair],
            out_specs=[whole(shape) for shape in shapes],
        ),
        out_shape=[jax.ShapeDtypeStruct(shape, bf16) for shape in shapes],
        name="join",
    )(place, *[value for pair in pairs for value in pair])


def unfold(place, heads, pieces, begun):
    shape = jax.ShapeDtypeStruct((heads, LATENT, NOPE), f32)
    parts = [part for _, *parts in pieces for part in parts]
    operands = parts + [swapped(part) for part in parts]
    sides = parts[0].shape[0]
    n_x = heads // (2 * sides)
    count = 2 * len(pieces) * sides

    def kernel(place, *refs):
        sources = list(refs[:len(operands)])
        key_out, value_out, keys, values, sems = refs[-5:]
        started = []
        for n in range(2 * len(pieces)):
            x_away, *part = pieces[n % len(pieces)]
            core = place[0] if n < len(pieces) else 1 - place[0]
            x = lax.rem(place[1] + x_away, n_x)
            part = [sources.pop(0) for _ in part]
            for side in range(sides):
                slot = n * sides + side
                start = 0
                for ref in part:
                    rows = slice(start, start + ref.shape[1])
                    keys[slot, rows, :] = ref[side, :, :NOPE].astype(f32)
                    values[slot, rows, :] = ref[side, :, NOPE:].astype(f32)
                    start += ref.shape[1]
                head = core * (heads // 2) + side * n_x + x
                for which, (done, out) in enumerate(((keys, key_out), (values, value_out))):
                    copy = pltpu.make_async_copy(done.at[slot], out.at[head], sems.at[which, slot])
                    copy.start()
                    started.append(copy)
        for copy in started:
            copy.wait()

    first = 1 + len(operands)
    return pl.pallas_call(
        kernel,
        grid_spec=pltpu.PrefetchScalarGridSpec(
            num_scalar_prefetch=1,
            grid=(1,),
            in_specs=[pl.BlockSpec(part.shape, lambda i, place: (0, 0, 0)) for part in operands]
            + [pl.BlockSpec(memory_space=pl.ANY)] * len(begun),
            out_specs=[pl.BlockSpec(memory_space=pl.ANY)] * 2,
            scratch_shapes=[pltpu.VMEM((count, LATENT, NOPE), f32)] * 2
            + [pltpu.SemaphoreType.DMA((2, count))],
        ),
        out_shape=[shape, shape],
        input_output_aliases={first: 0, first + 1: 1} if begun else {},
        name="unfold",
        compiler_params=pltpu.CompilerParams(vmem_limit_bytes=24 * MIB),
        cost_estimate=pl.CostEstimate(flops=0, bytes_accessed=4_000_000, transcendentals=0),
    )(place, *operands, *begun)


def pack(queries, n_head):
    rows, lanes = queries.shape
    lanes //= 2 * n_head

    def kernel(query_ref, out_ref):
        for head in range(n_head):
            for core in range(2):
                at = (2 * head + core) * lanes
                out_ref[core * n_head + head] = query_ref[:, at:at + lanes]

    return pl.pallas_call(
        kernel,
        out_shape=jax.ShapeDtypeStruct((2 * n_head, rows, lanes), bf16),
        name="pack",
    )(queries)


def swapped(value):
    return lax.ppermute(value, "core", [(0, 1), (1, 0)])


def shifted(value, axis, steps):
    count = lax.axis_size(axis)
    return lax.ppermute(value, axis, [(i, (i + steps) % count) for i in range(count)])


def exchanged(value, axes):
    return lax.all_to_all(value, axes, 0, 0, tiled=True)


def copies(value, count):
    return jnp.broadcast_to(value[None], (count,) + value.shape)


def added(*terms):
    return sum(term.astype(f32) for term in terms)


def folded(rows, axis):
    count = rows.shape[0]
    return added(rows[0], *[shifted(rows[s], axis, s) for s in range(1, count)])


def on_device(queries, latent, key_up, value_up, out_grad, block_docs):
    n_head = lax.axis_size(HEAD_AXES)
    n_x = lax.axis_size("x")
    core = lax.axis_index("core")
    x_here = lax.axis_index("x")
    n_z, n_y = [lax.axis_size(axis) for axis in HEAD_AXES]
    docs = block_docs[0]
    doc_first = [jnp.sum((docs < docs[2 * x_here + side]).astype(jnp.int32)) for side in range(2)]
    place = jnp.stack(
        [core, x_here] + [lax.axis_index(axis) for axis in HEAD_AXES] + doc_first
        + [lax.axis_index("dp")]
    ).astype(jnp.int32)

    half = out_grad.shape[1] // 2
    arrived = pack(queries, n_head)
    own = exchanged(copies(latent, n_head), HEAD_AXES)
    own, arrived, out_grad = lax.optimization_barrier((own, arrived, out_grad))
    arrived = exchanged(arrived, ("core",) + HEAD_AXES).reshape(2, BLOCK, -1)
    own = own.reshape(BLOCK, KEY)
    own = jnp.stack([own] + [shifted(own, "x", s) for s in range(1, n_x)])
    other = swapped(own)
    got_grad = swapped(lax.dynamic_slice_in_dim(out_grad, (1 - core) * half, half, 1))

    attended, query_grad, *kv, rows_keep, rows_send = attention(
        place, arrived, own, other, key_up, value_up, out_grad, got_grad, n_z, n_y
    )
    after = lax.optimization_barrier
    heads = key_up.shape[0]
    far_right, far_left, right_top, right_low, left_top, left_low, stay = kv
    past_right, past_left = shifted(far_right, "x", 1), shifted(far_left, "x", -1)
    low, top = shifted(right_low, "x", 1), shifted(left_top, "x", -1)
    rows = added(rows_keep, swapped(rows_send)).astype(bf16)
    from_left = shifted(added(right_top, past_right).astype(bf16), "x", 1)
    from_right = shifted(added(left_low, past_left).astype(bf16), "x", -1)
    upper = added(stay[:, :HALF], from_left, top)
    lower = added(stay[:, HALF:], from_right, low)
    kv = jnp.concatenate([upper, lower], axis=1).astype(bf16)
    kv, rows, attended, query_grad = after((kv, rows, attended, query_grad))
    kv = added(kv, shifted(kv, "dp", 1)).astype(bf16)
    rows = folded(rows, HEAD_AXES[0]).astype(bf16)
    got = swapped(attended[1]), swapped(query_grad[1])
    kv, rows, got = after((kv, rows, got))
    left, right = shifted(kv, "x", 1), shifted(kv, "x", -1)
    rows = folded(rows, HEAD_AXES[1]).astype(bf16)
    attended, query_grad = join(place, (attended[0], got[0]), (query_grad[0], got[1]))
    grads = unfold(place, heads, [(0, kv)], [])
    left, right, rows, attended, query_grad, grads = after(
        (left, right, rows, attended, query_grad, grads)
    )
    far = shifted(left[:, :HALF], "x", 1), shifted(right[:, HALF:], "x", -1)
    rows = [rows[0]] + [shifted(rows[s], "x", s) for s in range(1, n_x)]
    grads = unfold(place, heads, [(n_x - 1, left), (1, right)], grads)
    far, rows, grads = after((far, rows, grads))
    grads = unfold(place, heads, [(2,) + tuple(far)], grads)
    latent_grad = added(*rows)[:, :KEY]
    key_up_grad, value_up_grad = grads
    return (attended, query_grad, latent_grad, key_up_grad, value_up_grad)


def solution(mesh):
    n_dp, n_head, n_blk = mesh.devices.shape
    fine = Mesh(
        mesh.devices.reshape(n_dp, n_head // 2, 2, n_blk // 2, 2), ("dp", "z", "y", "x", "core")
    )
    head, blk = HEAD_AXES, ("x", "core")
    return jax.shard_map(
        on_device,
        mesh=fine,
        in_specs=(
            P(("dp",) + blk + head, None),
            P(("dp",) + blk + head, None),
            P(head, None, None),
            P(head, None, None),
            P(("dp",) + blk, head),
            P("dp", None),
        ),
        out_specs=(
            P(("dp",) + blk, head),
            P(("dp",) + blk, head),
            P(("dp",) + blk + head, None),
            P(head, None, None),
            P(head, None, None),
        ),
        check_vma=False,
    )
```

```python
import jax
import jax.numpy as jnp
from jax import lax
from jax.experimental import pallas as pl
from jax.experimental.pallas import tpu as pltpu
from jax.sharding import Mesh
from jax.sharding import PartitionSpec as P

NOPE = 128
ROPE = 64
LATENT = 512
VHEAD = 128
BLOCK = 128
QUERY = NOPE + ROPE
KEY = LATENT + ROPE
KEY_PAD = 640
HALF = LATENT // 2
DOC_MOST = 6
WINDOW = DOC_MOST * BLOCK
PAIR = 2
SCALE = QUERY ** -0.5
MIB = 1024 * 1024

bf16 = jnp.bfloat16
f32 = jnp.float32
NT = ((1,), (1,))
TN = ((0,), (0,))
HEAD_AXES = ("z", "y")


def mul(a, b, dims=((1,), (0,))):
    return lax.dot_general(a, b, (dims, ((), ())), preferred_element_type=f32)


def at_block(block):
    return pl.ds(pl.multiple_of(block * BLOCK, BLOCK), BLOCK)


def attention_kernel(
    place, docs, query_ref, own_ref, other_ref, key_ref, value_ref, grad_ref,
    back_ref, kv_ref, keep_ref, send_ref,
    keys, flipped, total, query_lat, context_grad, contexts, lat_grads,
):
    core, x_here, z_here, y_here = place[0], place[1], place[2], place[3]
    n_x = own_ref.shape[0]
    blocks = 2 * n_x
    pair = range(PAIR)
    doc_first = [
        sum([(docs[0, earlier] < docs[0, block]).astype(jnp.int32) for earlier in range(block)], 0)
        for block in range(blocks)
    ]
    for s in range(n_x):
        x = lax.rem(x_here + n_x - s, n_x)
        keys[at_block(2 * x + core), :] = own_ref[s]
        keys[at_block(2 * x + 1 - core), :] = other_ref[s]
    flipped[:LATENT, :] = jnp.transpose(keys[:, :LATENT])
    flipped[LATENT:, :] = jnp.transpose(keys[:, LATENT:])
    total[...] = jnp.zeros_like(total)

    slot = lambda block: (block % 2) * n_x + block // 2
    lanes = lambda block: slice(block * BLOCK, (block + 1) * BLOCK)
    columns = lambda block, e: slice((PAIR * block + e) * BLOCK, (PAIR * block + e + 1) * BLOCK)
    both = lambda block: slice(PAIR * block * BLOCK, PAIR * (block + 1) * BLOCK)
    nope = [query_ref[:, e * QUERY:e * QUERY + NOPE] for e in pair]
    grads = [
        jnp.concatenate(
            [grad_ref[slot(block), :, e * VHEAD:(e + 1) * VHEAD] for block in range(blocks)], axis=0
        )
        for e in pair
    ]
    for e in pair:
        spread_query = mul(key_ref[e], nope[e], NT).astype(bf16)
        spread_grad = mul(value_ref[e], grads[e], NT).astype(bf16)
        for block in range(blocks):
            query_lat[:, columns(block, e)] = spread_query[:, lanes(block)]
            context_grad[:, columns(block, e)] = spread_grad[:, lanes(block)]

    def window_of(block):
        return slice(max(block + 1 - DOC_MOST, 0) * BLOCK, (block + 1) * BLOCK)

    def turned_of(block):
        return jnp.concatenate(
            [query_ref[lanes(block), e * QUERY + NOPE:(e + 1) * QUERY] for e in pair], axis=0
        )

    def scores_of(block):
        window = window_of(block)
        shape = (window.stop - window.start, BLOCK)
        key_at = window.start + lax.broadcasted_iota(jnp.int32, shape, 0)
        query_at = block * BLOCK + lax.broadcasted_iota(jnp.int32, shape, 1)
        seen = (key_at >= doc_first[block] * BLOCK) & (key_at <= query_at)
        hidden = jnp.concatenate([jnp.where(seen, f32(0.0), f32(-1e30))] * PAIR, axis=1)
        near = mul(keys[window, :LATENT], query_lat[:, both(block)])
        return (near + mul(keys[window, LATENT:], turned_of(block), NT)) * SCALE + hidden

    def softmax_of(scores):
        top = jnp.max(scores, axis=0, keepdims=True)
        expo = jnp.exp(scores - top)
        return expo, 1.0 / jnp.sum(expo, axis=0, keepdims=True)

    def context_of(block, expo, inverse):
        context = (mul(flipped[:LATENT, window_of(block)], expo.astype(bf16)) * inverse).astype(bf16)
        delta = jnp.sum(
            context.astype(f32) * context_grad[:, both(block)].astype(f32), axis=0, keepdims=True
        )
        return context, delta

    def score_grad_of(block, expo, inverse, delta):
        probs = expo * inverse
        grad = mul(keys[window_of(block), :LATENT], context_grad[:, both(block)]) - delta
        return (probs * grad * SCALE).astype(bf16), probs.astype(bf16)

    def lat_grad_of(block, score_grad, low):
        window = window_of(block)
        lat_grad = mul(flipped[:, window], score_grad)
        total[window, :LATENT] += mul(score_grad, query_lat[:, both(block)], NT) + mul(
            low, context_grad[:, both(block)], NT
        )
        total[window, LATENT:] += mul(score_grad, turned_of(block))
        return lat_grad[:LATENT, :].astype(bf16), lat_grad[LATENT:, :]

    def finish(block, context, lat_grad, turned_grad):
        pieces = []
        for e in pair:
            at = slice(e * BLOCK, (e + 1) * BLOCK)
            contexts[e, :, lanes(block)] = context[:, at]
            lat_grads[e, :, lanes(block)] = lat_grad[:, at]
            back_ref[slot(block), :, e * VHEAD:(e + 1) * VHEAD] = mul(
                context[:, at], value_ref[e], TN
            ).astype(bf16)
            pieces.append(mul(lat_grad[:, at], key_ref[e], TN))
            pieces.append(jnp.transpose(turned_grad[:, at]))
        back_ref[slot(block), :, PAIR * VHEAD:] = jnp.concatenate(pieces, axis=1).astype(bf16)

    for low_block in range(blocks // 2):
        duo = (blocks - 1 - low_block, low_block)
        scores = [scores_of(block) for block in duo]
        soft = [softmax_of(score) for score in scores]
        done = [context_of(block, *soft[n]) for n, block in enumerate(duo)]
        score_grads = [
            score_grad_of(block, *soft[n], done[n][1]) for n, block in enumerate(duo)
        ]
        last = [lat_grad_of(block, *score_grads[n]) for n, block in enumerate(duo)]
        for n, block in enumerate(duo):
            finish(block, done[n][0], *last[n])

    for e in pair:
        kv_ref[e, :, :NOPE] = mul(lat_grads[e], nope[e]).astype(bf16)
        kv_ref[e, :, NOPE:] = mul(contexts[e], grads[e]).astype(bf16)

    n_z, n_y, _, rows = keep_ref.shape[:4]
    empty = jnp.zeros((rows, KEY_PAD - KEY), bf16)
    for dz in range(n_z):
        for dy in range(n_y):
            head = lax.rem(z_here + dz, n_z) * n_y + lax.rem(y_here + dy, n_y)
            for dx in range(n_x):
                x = lax.rem(x_here + dx, n_x)
                for ref, parity in ((keep_ref, core), (send_ref, 1 - core)):
                    start = pl.multiple_of((2 * x + parity) * BLOCK + head * rows, rows)
                    ref[dz, dy, dx, :, :KEY] = total[pl.ds(start, rows), :].astype(bf16)
                    ref[dz, dy, dx, :, KEY:] = empty


def attention(place, docs, queries, own, other, key_up, value_up, grads, n_z, n_y):
    n_x = own.shape[0]
    tokens = 2 * n_x * BLOCK
    whole = lambda shape: pl.BlockSpec(shape, lambda i, place, docs: (0,) * len(shape))
    weights = pl.BlockSpec((PAIR, LATENT, NOPE), lambda i, place, docs: (place[0] * n_x + place[1], 0, 0))
    rows_shape = (n_z, n_y, n_x, BLOCK // (n_z * n_y), KEY_PAD)
    out_shapes = [
        (2 * n_x, BLOCK, PAIR * (VHEAD + QUERY)),
        (PAIR, LATENT, NOPE + VHEAD),
        rows_shape,
        rows_shape,
    ]
    return pl.pallas_call(
        attention_kernel,
        grid_spec=pltpu.PrefetchScalarGridSpec(
            num_scalar_prefetch=2,
            grid=(1,),
            in_specs=[
                whole(queries.shape),
                whole(own.shape),
                whole(other.shape),
                weights,
                weights,
                whole(grads.shape),
            ],
            out_specs=[whole(shape) for shape in out_shapes],
            scratch_shapes=[
                pltpu.VMEM((tokens, KEY), bf16),
                pltpu.VMEM((KEY, tokens), bf16),
                pltpu.VMEM((tokens, KEY), f32),
                pltpu.VMEM((LATENT, PAIR * tokens), bf16),
                pltpu.VMEM((LATENT, PAIR * tokens), bf16),
                pltpu.VMEM((PAIR, LATENT, tokens), bf16),
                pltpu.VMEM((PAIR, LATENT, tokens), bf16),
            ],
        ),
        out_shape=[jax.ShapeDtypeStruct(shape, bf16) for shape in out_shapes],
        name="attention",
        compiler_params=pltpu.CompilerParams(
            dimension_semantics=("arbitrary",), vmem_limit_bytes=48 * MIB
        ),
        cost_estimate=pl.CostEstimate(
            flops=9_000_000_000, bytes_accessed=15_000_000, transcendentals=1_600_000
        ),
    )(place, docs, queries, own, other, key_up, value_up, grads)


def join(back):
    slots, rows, width = back.shape
    value = PAIR * VHEAD

    def kernel(back_ref, attended_ref, query_grad_ref):
        for n in range(slots):
            attended_ref[:, n * value:(n + 1) * value] = back_ref[n, :, :value]
            at = slice(n * (width - value), (n + 1) * (width - value))
            query_grad_ref[:, at] = back_ref[n, :, value:]

    return pl.pallas_call(
        kernel,
        out_shape=[
            jax.ShapeDtypeStruct((rows, slots * value), bf16),
            jax.ShapeDtypeStruct((rows, slots * (width - value)), bf16),
        ],
        name="join",
    )(back)


def unfold(place, heads, pieces, begun):
    shape = jax.ShapeDtypeStruct((heads, LATENT, NOPE), f32)
    parts = [part for _, *parts in pieces for part in parts]
    operands = parts + [swapped(part) for part in parts]
    sides = parts[0].shape[0]
    n_x = heads // (2 * sides)
    count = 2 * len(pieces) * sides

    def kernel(place, *refs):
        sources = list(refs[:len(operands)])
        key_out, value_out, keys, values, sems = refs[-5:]
        started = []
        for n in range(2 * len(pieces)):
            x_away, *part = pieces[n % len(pieces)]
            core = place[0] if n < len(pieces) else 1 - place[0]
            x = lax.rem(place[1] + x_away, n_x)
            part = [sources.pop(0) for _ in part]
            for side in range(sides):
                slot = n * sides + side
                start = 0
                for ref in part:
                    rows = slice(start, start + ref.shape[1])
                    keys[slot, rows, :] = ref[side, :, :NOPE].astype(f32)
                    values[slot, rows, :] = ref[side, :, NOPE:].astype(f32)
                    start += ref.shape[1]
                head = core * (heads // 2) + x * sides + side
                for which, (done, out) in enumerate(((keys, key_out), (values, value_out))):
                    copy = pltpu.make_async_copy(done.at[slot], out.at[head], sems.at[which, slot])
                    copy.start()
                    started.append(copy)
        for copy in started:
            copy.wait()

    first = 1 + len(operands)
    return pl.pallas_call(
        kernel,
        grid_spec=pltpu.PrefetchScalarGridSpec(
            num_scalar_prefetch=1,
            grid=(1,),
            in_specs=[pl.BlockSpec(part.shape, lambda i, place: (0, 0, 0)) for part in operands]
            + [pl.BlockSpec(memory_space=pl.ANY)] * len(begun),
            out_specs=[pl.BlockSpec(memory_space=pl.ANY)] * 2,
            scratch_shapes=[pltpu.VMEM((count, LATENT, NOPE), f32)] * 2
            + [pltpu.SemaphoreType.DMA((2, count))],
        ),
        out_shape=[shape, shape],
        input_output_aliases={first: 0, first + 1: 1} if begun else {},
        name="unfold",
        compiler_params=pltpu.CompilerParams(vmem_limit_bytes=24 * MIB),
        cost_estimate=pl.CostEstimate(flops=0, bytes_accessed=4_000_000, transcendentals=0),
    )(place, *operands, *begun)


def pack(queries, n_head, n_x):
    rows, lanes = queries.shape
    lanes //= 2 * n_head * n_x

    def kernel(query_ref, out_ref):
        for head in range(n_head):
            for core in range(2):
                for x in range(n_x):
                    at = ((head * 2 + core) * n_x + x) * lanes
                    out_ref[(x * 2 + core) * n_head + head] = query_ref[:, at:at + lanes]

    return pl.pallas_call(
        kernel,
        out_shape=jax.ShapeDtypeStruct((2 * n_head * n_x, rows, lanes), bf16),
        name="pack",
    )(queries)


def swapped(value):
    return lax.ppermute(value, "core", [(0, 1), (1, 0)])


def shifted(value, axis, steps):
    count = lax.axis_size(axis)
    return lax.ppermute(value, axis, [(i, (i + steps) % count) for i in range(count)])


def exchanged(value, axes):
    return lax.all_to_all(value, axes, 0, 0, tiled=True)


def copies(value, count):
    return jnp.broadcast_to(value[None], (count,) + value.shape)


def added(*terms):
    return sum(term.astype(f32) for term in terms)


def folded(rows, axis):
    count = rows.shape[0]
    return added(rows[0], *[shifted(rows[s], axis, s) for s in range(1, count)])


def on_device(queries, latent, key_up, value_up, out_grad, block_docs):
    n_head = lax.axis_size(HEAD_AXES)
    n_x = lax.axis_size("x")
    core = lax.axis_index("core")
    x_here = lax.axis_index("x")
    n_z, n_y = [lax.axis_size(axis) for axis in HEAD_AXES]
    place = jnp.stack(
        [core, x_here] + [lax.axis_index(axis) for axis in HEAD_AXES]
    ).astype(jnp.int32)

    heads = key_up.shape[0]
    fine_axes = ("core", "x")
    grads = jnp.swapaxes(out_grad.reshape(BLOCK, 2 * n_x, -1), 0, 1)
    arrived = pack(queries, n_head, n_x)
    own = exchanged(copies(latent, n_head), HEAD_AXES)
    own, arrived = lax.optimization_barrier((own, arrived))
    arrived = exchanged(arrived, ("x", "core") + HEAD_AXES).reshape(2 * n_x * BLOCK, -1)
    own = own.reshape(BLOCK, KEY)
    own = jnp.stack([own] + [shifted(own, "x", s) for s in range(1, n_x)])
    other = swapped(own)
    grads = exchanged(grads, fine_axes)

    back, kv, rows_keep, rows_send = attention(
        place, block_docs, arrived, own, other, key_up, value_up, grads, n_z, n_y
    )
    after = lax.optimization_barrier
    rows = added(rows_keep, swapped(rows_send)).astype(bf16)
    back = exchanged(back, fine_axes)
    kv = added(kv, shifted(kv, "dp", 1)).astype(bf16)
    rows = folded(rows, HEAD_AXES[0]).astype(bf16)
    kv, back = after((kv, back))
    upper, lower = kv[:, :HALF], kv[:, HALF:]
    before = [shifted(upper, "x", 1), shifted(lower, "x", 1)]
    behind = [shifted(lower, "x", -1), shifted(upper, "x", -1)]
    rows = folded(rows, HEAD_AXES[1]).astype(bf16)
    grads = unfold(place, heads, [(0, kv)], [])
    attended, query_grad = join(back)
    before[0], behind[0], rows, grads, attended, query_grad = after(
        (before[0], behind[0], rows, grads, attended, query_grad)
    )
    far = shifted(before[0], "x", 1), shifted(behind[0], "x", -1)
    rows = [rows[0]] + [shifted(rows[s], "x", s) for s in range(1, n_x)]
    grads = unfold(place, heads, [(n_x - 1, *before), (1, *behind[::-1])], grads)
    far, rows, grads, attended, query_grad = after((far, rows, grads, attended, query_grad))
    grads = unfold(place, heads, [(2,) + tuple(far)], grads)
    latent_grad = added(*rows)[:, :KEY]
    key_up_grad, value_up_grad = grads
    return (attended, query_grad, latent_grad, key_up_grad, value_up_grad)


def solution(mesh):
    n_dp, n_head, n_blk = mesh.devices.shape
    fine = Mesh(
        mesh.devices.reshape(n_dp, n_head // 2, 2, n_blk // 2, 2), ("dp", "z", "y", "x", "core")
    )
    head, blk = HEAD_AXES, ("x", "core")
    return jax.shard_map(
        on_device,
        mesh=fine,
        in_specs=(
            P(("dp",) + blk + head, None),
            P(("dp",) + blk + head, None),
            P(head, None, None),
            P(head, None, None),
            P(("dp",) + blk, head),
            P("dp", None),
        ),
        out_specs=(
            P(("dp",) + blk, head),
            P(("dp",) + blk, head),
            P(("dp",) + blk + head, None),
            P(head, None, None),
            P(head, None, None),
        ),
        check_vma=False,
    )
```

```python
import jax
import jax.numpy as jnp
from jax import lax
from jax.experimental import pallas as pl
from jax.experimental.pallas import tpu as pltpu
from jax.sharding import Mesh
from jax.sharding import PartitionSpec as P

NOPE = 128
ROPE = 64
LATENT = 512
VHEAD = 128
BLOCK = 128
QUERY = NOPE + ROPE
KEY = LATENT + ROPE
KEY_PAD = 640
HALF = LATENT // 2
DOC_MOST = 6
WINDOW = DOC_MOST * BLOCK
PAIR = 2
SCALE = QUERY ** -0.5
MIB = 1024 * 1024

bf16 = jnp.bfloat16
f32 = jnp.float32
NT = ((1,), (1,))
TN = ((0,), (0,))
HEAD_AXES = ("z", "y")


def mul(a, b, dims=((1,), (0,))):
    return lax.dot_general(a, b, (dims, ((), ())), preferred_element_type=f32)


def at_block(block):
    return pl.ds(pl.multiple_of(block * BLOCK, BLOCK), BLOCK)


def attention_kernel(
    place, docs, query_ref, own_ref, other_ref, key_ref, value_ref, grad_ref,
    back_ref, kv_ref, keep_ref, send_ref,
    keys, flipped, total, query_lat, context_grad, contexts, lat_grads,
):
    core, x_here, z_here, y_here = place[0], place[1], place[2], place[3]
    n_x = own_ref.shape[0]
    blocks = 2 * n_x
    pair = range(PAIR)
    doc_first = [
        sum([(docs[0, earlier] < docs[0, block]).astype(jnp.int32) for earlier in range(block)], 0)
        for block in range(blocks)
    ]
    for s in range(n_x):
        x = lax.rem(x_here + n_x - s, n_x)
        n_z, n_y, _, rows = keep_ref.shape[:4]
        for dz in range(n_z):
            for dy in range(n_y):
                head = lax.rem(z_here + n_z - dz, n_z) * n_y + lax.rem(y_here + n_y - dy, n_y)
                at_row = (dy * n_z + dz) * rows
                for ref, parity in ((own_ref, core), (other_ref, 1 - core)):
                    start = pl.multiple_of((2 * x + parity) * BLOCK + head * rows, rows)
                    keys[pl.ds(start, rows), :] = ref[s, at_row:at_row + rows, :]
    flipped[:LATENT, :] = jnp.transpose(keys[:, :LATENT])
    flipped[LATENT:, :] = jnp.transpose(keys[:, LATENT:])
    total[...] = jnp.zeros_like(total)

    slot = lambda block: (block % 2) * n_x + block // 2
    lanes = lambda block: slice(block * BLOCK, (block + 1) * BLOCK)
    columns = lambda block, e: slice((PAIR * block + e) * BLOCK, (PAIR * block + e + 1) * BLOCK)
    both = lambda block: slice(PAIR * block * BLOCK, PAIR * (block + 1) * BLOCK)
    nope = [query_ref[:, e * QUERY:e * QUERY + NOPE] for e in pair]
    grads = [
        jnp.concatenate(
            [grad_ref[slot(block), :, e * VHEAD:(e + 1) * VHEAD] for block in range(blocks)], axis=0
        )
        for e in pair
    ]
    for e in pair:
        spread_query = mul(key_ref[e], nope[e], NT).astype(bf16)
        spread_grad = mul(value_ref[e], grads[e], NT).astype(bf16)
        for block in range(blocks):
            query_lat[:, columns(block, e)] = spread_query[:, lanes(block)]
            context_grad[:, columns(block, e)] = spread_grad[:, lanes(block)]

    def window_of(block):
        return slice(max(block + 1 - DOC_MOST, 0) * BLOCK, (block + 1) * BLOCK)

    def turned_of(block):
        return jnp.concatenate(
            [query_ref[lanes(block), e * QUERY + NOPE:(e + 1) * QUERY] for e in pair], axis=0
        )

    def scores_of(block):
        window = window_of(block)
        shape = (window.stop - window.start, BLOCK)
        key_at = window.start + lax.broadcasted_iota(jnp.int32, shape, 0)
        query_at = block * BLOCK + lax.broadcasted_iota(jnp.int32, shape, 1)
        seen = (key_at >= doc_first[block] * BLOCK) & (key_at <= query_at)
        hidden = jnp.concatenate([jnp.where(seen, f32(0.0), f32(-1e30))] * PAIR, axis=1)
        near = mul(keys[window, :LATENT], query_lat[:, both(block)])
        return (near + mul(keys[window, LATENT:], turned_of(block), NT)) * SCALE + hidden

    def softmax_of(scores):
        top = jnp.max(scores, axis=0, keepdims=True)
        expo = jnp.exp(scores - top)
        return expo, 1.0 / jnp.sum(expo, axis=0, keepdims=True)

    def context_of(block, expo, inverse):
        context = (mul(flipped[:LATENT, window_of(block)], expo.astype(bf16)) * inverse).astype(bf16)
        delta = jnp.sum(
            context.astype(f32) * context_grad[:, both(block)].astype(f32), axis=0, keepdims=True
        )
        return context, delta

    def score_grad_of(block, expo, inverse, delta):
        probs = expo * inverse
        grad = mul(keys[window_of(block), :LATENT], context_grad[:, both(block)]) - delta
        return (probs * grad * SCALE).astype(bf16), probs.astype(bf16)

    def lat_grad_of(block, score_grad, low):
        window = window_of(block)
        lat_grad = mul(flipped[:, window], score_grad)
        total[window, :LATENT] += mul(score_grad, query_lat[:, both(block)], NT) + mul(
            low, context_grad[:, both(block)], NT
        )
        total[window, LATENT:] += mul(score_grad, turned_of(block))
        return lat_grad[:LATENT, :].astype(bf16), lat_grad[LATENT:, :]

    def finish(block, context, lat_grad, turned_grad):
        pieces = []
        for e in pair:
            at = slice(e * BLOCK, (e + 1) * BLOCK)
            contexts[e, :, lanes(block)] = context[:, at]
            lat_grads[e, :, lanes(block)] = lat_grad[:, at]
            back_ref[slot(block), :, e * VHEAD:(e + 1) * VHEAD] = mul(
                context[:, at], value_ref[e], TN
            ).astype(bf16)
            pieces.append(mul(lat_grad[:, at], key_ref[e], TN))
            pieces.append(jnp.transpose(turned_grad[:, at]))
        back_ref[slot(block), :, PAIR * VHEAD:] = jnp.concatenate(pieces, axis=1).astype(bf16)

    for low_block in range(blocks // 2):
        duo = (blocks - 1 - low_block, low_block)
        scores = [scores_of(block) for block in duo]
        soft = [softmax_of(score) for score in scores]
        done = [context_of(block, *soft[n]) for n, block in enumerate(duo)]
        score_grads = [
            score_grad_of(block, *soft[n], done[n][1]) for n, block in enumerate(duo)
        ]
        last = [lat_grad_of(block, *score_grads[n]) for n, block in enumerate(duo)]
        for n, block in enumerate(duo):
            finish(block, done[n][0], *last[n])

    for e in pair:
        kv_ref[e, :, :NOPE] = mul(lat_grads[e], nope[e]).astype(bf16)
        kv_ref[e, :, NOPE:] = mul(contexts[e], grads[e]).astype(bf16)

    n_z, n_y, _, rows = keep_ref.shape[:4]
    empty = jnp.zeros((rows, KEY_PAD - KEY), bf16)
    for dz in range(n_z):
        for dy in range(n_y):
            head = lax.rem(z_here + dz, n_z) * n_y + lax.rem(y_here + dy, n_y)
            for dx in range(n_x):
                x = lax.rem(x_here + dx, n_x)
                for ref, parity in ((keep_ref, core), (send_ref, 1 - core)):
                    start = pl.multiple_of((2 * x + parity) * BLOCK + head * rows, rows)
                    ref[dz, dy, dx, :, :KEY] = total[pl.ds(start, rows), :].astype(bf16)
                    ref[dz, dy, dx, :, KEY:] = empty


def attention(place, docs, queries, own, other, key_up, value_up, grads, n_z, n_y):
    n_x = own.shape[0]
    tokens = 2 * n_x * BLOCK
    whole = lambda shape: pl.BlockSpec(shape, lambda i, place, docs: (0,) * len(shape))
    weights = pl.BlockSpec((PAIR, LATENT, NOPE), lambda i, place, docs: (place[0] * n_x + place[1], 0, 0))
    rows_shape = (n_z, n_y, n_x, BLOCK // (n_z * n_y), KEY_PAD)
    out_shapes = [
        (2 * n_x, BLOCK, PAIR * (VHEAD + QUERY)),
        (PAIR, LATENT, NOPE + VHEAD),
        rows_shape,
        rows_shape,
    ]
    return pl.pallas_call(
        attention_kernel,
        grid_spec=pltpu.PrefetchScalarGridSpec(
            num_scalar_prefetch=2,
            grid=(1,),
            in_specs=[
                whole(queries.shape),
                whole(own.shape),
                whole(other.shape),
                weights,
                weights,
                whole(grads.shape),
            ],
            out_specs=[whole(shape) for shape in out_shapes],
            scratch_shapes=[
                pltpu.VMEM((tokens, KEY), bf16),
                pltpu.VMEM((KEY, tokens), bf16),
                pltpu.VMEM((tokens, KEY), f32),
                pltpu.VMEM((LATENT, PAIR * tokens), bf16),
                pltpu.VMEM((LATENT, PAIR * tokens), bf16),
                pltpu.VMEM((PAIR, LATENT, tokens), bf16),
                pltpu.VMEM((PAIR, LATENT, tokens), bf16),
            ],
        ),
        out_shape=[jax.ShapeDtypeStruct(shape, bf16) for shape in out_shapes],
        name="attention",
        compiler_params=pltpu.CompilerParams(
            dimension_semantics=("arbitrary",), vmem_limit_bytes=48 * MIB
        ),
        cost_estimate=pl.CostEstimate(
            flops=9_000_000_000, bytes_accessed=15_000_000, transcendentals=1_600_000
        ),
    )(place, docs, queries, own, other, key_up, value_up, grads)


def join(back):
    slots, rows, width = back.shape
    value = PAIR * VHEAD

    def kernel(back_ref, attended_ref, query_grad_ref):
        for n in range(slots):
            attended_ref[:, n * value:(n + 1) * value] = back_ref[n, :, :value]
            at = slice(n * (width - value), (n + 1) * (width - value))
            query_grad_ref[:, at] = back_ref[n, :, value:]

    return pl.pallas_call(
        kernel,
        out_shape=[
            jax.ShapeDtypeStruct((rows, slots * value), bf16),
            jax.ShapeDtypeStruct((rows, slots * (width - value)), bf16),
        ],
        name="join",
    )(back)


def unfold(place, heads, pieces, begun):
    shape = jax.ShapeDtypeStruct((heads, LATENT, NOPE), f32)
    parts = [part for _, *parts in pieces for part in parts]
    operands = parts + [swapped(part) for part in parts]
    sides = parts[0].shape[0]
    n_x = heads // (2 * sides)
    count = 2 * len(pieces) * sides

    def kernel(place, *refs):
        sources = list(refs[:len(operands)])
        key_out, value_out, keys, values, sems = refs[-5:]
        started = []
        for n in range(2 * len(pieces)):
            x_away, *part = pieces[n % len(pieces)]
            core = place[0] if n < len(pieces) else 1 - place[0]
            x = lax.rem(place[1] + x_away, n_x)
            part = [sources.pop(0) for _ in part]
            for side in range(sides):
                slot = n * sides + side
                start = 0
                for ref in part:
                    rows = slice(start, start + ref.shape[1])
                    keys[slot, rows, :] = ref[side, :, :NOPE].astype(f32)
                    values[slot, rows, :] = ref[side, :, NOPE:].astype(f32)
                    start += ref.shape[1]
                head = core * (heads // 2) + x * sides + side
                for which, (done, out) in enumerate(((keys, key_out), (values, value_out))):
                    copy = pltpu.make_async_copy(done.at[slot], out.at[head], sems.at[which, slot])
                    copy.start()
                    started.append(copy)
        for copy in started:
            copy.wait()

    first = 1 + len(operands)
    return pl.pallas_call(
        kernel,
        grid_spec=pltpu.PrefetchScalarGridSpec(
            num_scalar_prefetch=1,
            grid=(1,),
            in_specs=[pl.BlockSpec(part.shape, lambda i, place: (0, 0, 0)) for part in operands]
            + [pl.BlockSpec(memory_space=pl.ANY)] * len(begun),
            out_specs=[pl.BlockSpec(memory_space=pl.ANY)] * 2,
            scratch_shapes=[pltpu.VMEM((count, LATENT, NOPE), f32)] * 2
            + [pltpu.SemaphoreType.DMA((2, count))],
        ),
        out_shape=[shape, shape],
        input_output_aliases={first: 0, first + 1: 1} if begun else {},
        name="unfold",
        compiler_params=pltpu.CompilerParams(vmem_limit_bytes=24 * MIB),
        cost_estimate=pl.CostEstimate(flops=0, bytes_accessed=4_000_000, transcendentals=0),
    )(place, *operands, *begun)


def pack(queries, n_head, n_x):
    rows, lanes = queries.shape
    lanes //= 2 * n_head * n_x

    def kernel(query_ref, out_ref):
        for head in range(n_head):
            for core in range(2):
                for x in range(n_x):
                    at = ((head * 2 + core) * n_x + x) * lanes
                    out_ref[(x * 2 + core) * n_head + head] = query_ref[:, at:at + lanes]

    return pl.pallas_call(
        kernel,
        out_shape=jax.ShapeDtypeStruct((2 * n_head * n_x, rows, lanes), bf16),
        name="pack",
    )(queries)


def swapped(value):
    return lax.ppermute(value, "core", [(0, 1), (1, 0)])


def shifted(value, axis, steps):
    count = lax.axis_size(axis)
    return lax.ppermute(value, axis, [(i, (i + steps) % count) for i in range(count)])


def exchanged(value, axes):
    return lax.all_to_all(value, axes, 0, 0, tiled=True)


def copies(value, count):
    return jnp.broadcast_to(value[None], (count,) + value.shape)


def added(*terms):
    return sum(term.astype(f32) for term in terms)


def folded(rows, axis):
    count = rows.shape[0]
    return added(rows[0], *[shifted(rows[s], axis, s) for s in range(1, count)])


def on_device(queries, latent, key_up, value_up, out_grad, block_docs):
    n_head = lax.axis_size(HEAD_AXES)
    n_x = lax.axis_size("x")
    core = lax.axis_index("core")
    x_here = lax.axis_index("x")
    n_z, n_y = [lax.axis_size(axis) for axis in HEAD_AXES]
    place = jnp.stack(
        [core, x_here] + [lax.axis_index(axis) for axis in HEAD_AXES]
    ).astype(jnp.int32)

    heads = key_up.shape[0]
    fine_axes = ("core", "x")
    grads = jnp.swapaxes(out_grad.reshape(BLOCK, 2 * n_x, -1), 0, 1)
    arrived = pack(queries, n_head, n_x)
    own = jnp.stack([latent] + [shifted(latent, "z", s) for s in range(1, n_z)])
    own, grads = lax.optimization_barrier((own, grads))
    grads = exchanged(grads, fine_axes)
    own = jnp.stack([own] + [shifted(own, "y", s) for s in range(1, n_y)]).reshape(BLOCK, KEY)
    own, arrived = lax.optimization_barrier((own, arrived))
    grads, arrived = lax.optimization_barrier((grads, arrived))
    arrived = exchanged(arrived, ("x", "core") + HEAD_AXES).reshape(2 * n_x * BLOCK, -1)
    own = jnp.stack([own] + [shifted(own, "x", s) for s in range(1, n_x)])
    other = swapped(own)

    back, kv, rows_keep, rows_send = attention(
        place, block_docs, arrived, own, other, key_up, value_up, grads, n_z, n_y
    )
    after = lax.optimization_barrier
    rows = added(rows_keep, swapped(rows_send)).astype(bf16)
    back = exchanged(back, fine_axes)
    kv = added(kv, shifted(kv, "dp", 1)).astype(bf16)
    rows = folded(rows, HEAD_AXES[0]).astype(bf16)
    kv, back = after((kv, back))
    upper, lower = kv[:, :HALF], kv[:, HALF:]
    before = [shifted(upper, "x", 1), shifted(lower, "x", 1)]
    behind = [shifted(lower, "x", -1), shifted(upper, "x", -1)]
    rows = folded(rows, HEAD_AXES[1]).astype(bf16)
    grads = unfold(place, heads, [(0, kv)], [])
    attended, query_grad = join(back)
    before[0], behind[0], rows, grads, attended, query_grad = after(
        (before[0], behind[0], rows, grads, attended, query_grad)
    )
    far = shifted(before[0], "x", 1), shifted(behind[0], "x", -1)
    rows = [rows[0]] + [shifted(rows[s], "x", s) for s in range(1, n_x)]
    grads = unfold(place, heads, [(n_x - 1, *before), (1, *behind[::-1])], grads)
    far, rows, grads, attended, query_grad = after((far, rows, grads, attended, query_grad))
    grads = unfold(place, heads, [(2,) + tuple(far)], grads)
    latent_grad = added(*rows)[:, :KEY]
    key_up_grad, value_up_grad = grads
    return (attended, query_grad, latent_grad, key_up_grad, value_up_grad)


def solution(mesh):
    n_dp, n_head, n_blk = mesh.devices.shape
    fine = Mesh(
        mesh.devices.reshape(n_dp, n_head // 2, 2, n_blk // 2, 2), ("dp", "z", "y", "x", "core")
    )
    head, blk = HEAD_AXES, ("x", "core")
    return jax.shard_map(
        on_device,
        mesh=fine,
        in_specs=(
            P(("dp",) + blk + head, None),
            P(("dp",) + blk + head, None),
            P(head, None, None),
            P(head, None, None),
            P(("dp",) + blk, head),
            P("dp", None),
        ),
        out_specs=(
            P(("dp",) + blk, head),
            P(("dp",) + blk, head),
            P(("dp",) + blk + head, None),
            P(head, None, None),
            P(head, None, None),
        ),
        check_vma=False,
    )
```

```python
import jax
import jax.numpy as jnp
from jax import lax
from jax.experimental import pallas as pl
from jax.experimental.pallas import tpu as pltpu
from jax.sharding import Mesh
from jax.sharding import PartitionSpec as P

NOPE = 128
ROPE = 64
LATENT = 512
VHEAD = 128
BLOCK = 128
QUERY = NOPE + ROPE
KEY = LATENT + ROPE
KEY_PAD = 640
HALF = LATENT // 2
DOC_MOST = 6
WINDOW = DOC_MOST * BLOCK
PAIR = 2
SCALE = QUERY ** -0.5
MIB = 1024 * 1024

bf16 = jnp.bfloat16
f32 = jnp.float32
NT = ((1,), (1,))
TN = ((0,), (0,))
HEAD_AXES = ("z", "y")


def mul(a, b, dims=((1,), (0,))):
    return lax.dot_general(a, b, (dims, ((), ())), preferred_element_type=f32)


def at_block(block):
    return pl.ds(pl.multiple_of(block * BLOCK, BLOCK), BLOCK)


def attention_kernel(
    place, docs, query_ref, own_ref, other_ref, key_ref, value_ref, grad_ref,
    back_ref, kv_ref, keep_ref, send_ref,
    keys, flipped, total, query_lat, context_grad, contexts, lat_grads,
):
    core, x_here, z_here, y_here = place[0], place[1], place[2], place[3]
    n_x = own_ref.shape[0]
    blocks = 2 * n_x
    pair = range(PAIR)
    doc_first = [
        sum([(docs[0, earlier] < docs[0, block]).astype(jnp.int32) for earlier in range(block)], 0)
        for block in range(blocks)
    ]
    for s in range(n_x):
        x = lax.rem(x_here + n_x - s, n_x)
        n_z, n_y, _, rows = keep_ref.shape[:4]
        for dz in range(n_z):
            for dy in range(n_y):
                head = lax.rem(z_here + n_z - dz, n_z) * n_y + lax.rem(y_here + n_y - dy, n_y)
                at_row = (dy * n_z + dz) * rows
                for ref, parity in ((own_ref, core), (other_ref, 1 - core)):
                    start = pl.multiple_of((2 * x + parity) * BLOCK + head * rows, rows)
                    keys[pl.ds(start, rows), :] = ref[s, at_row:at_row + rows, :]
    flipped[:LATENT, :] = jnp.transpose(keys[:, :LATENT])
    flipped[LATENT:, :] = jnp.transpose(keys[:, LATENT:])
    total[...] = jnp.zeros_like(total)

    slot = lambda block: (block % 2) * n_x + block // 2
    lanes = lambda block: slice(block * BLOCK, (block + 1) * BLOCK)
    columns = lambda block, e: slice((PAIR * block + e) * BLOCK, (PAIR * block + e + 1) * BLOCK)
    both = lambda block: slice(PAIR * block * BLOCK, PAIR * (block + 1) * BLOCK)
    nope = [query_ref[:, e * QUERY:e * QUERY + NOPE] for e in pair]
    grads = [
        jnp.concatenate(
            [grad_ref[slot(block), :, e * VHEAD:(e + 1) * VHEAD] for block in range(blocks)], axis=0
        )
        for e in pair
    ]
    for e in pair:
        spread_query = mul(key_ref[e], nope[e], NT).astype(bf16)
        spread_grad = mul(value_ref[e], grads[e], NT).astype(bf16)
        for block in range(blocks):
            query_lat[:, columns(block, e)] = spread_query[:, lanes(block)]
            context_grad[:, columns(block, e)] = spread_grad[:, lanes(block)]

    def window_of(block):
        return slice(max(block + 1 - DOC_MOST, 0) * BLOCK, (block + 1) * BLOCK)

    def turned_of(block):
        return jnp.concatenate(
            [query_ref[lanes(block), e * QUERY + NOPE:(e + 1) * QUERY] for e in pair], axis=0
        )

    def scores_of(block):
        window = window_of(block)
        shape = (window.stop - window.start, BLOCK)
        key_at = window.start + lax.broadcasted_iota(jnp.int32, shape, 0)
        query_at = block * BLOCK + lax.broadcasted_iota(jnp.int32, shape, 1)
        seen = (key_at >= doc_first[block] * BLOCK) & (key_at <= query_at)
        hidden = jnp.concatenate([jnp.where(seen, f32(0.0), f32(-1e30))] * PAIR, axis=1)
        near = mul(keys[window, :LATENT], query_lat[:, both(block)])
        return (near + mul(keys[window, LATENT:], turned_of(block), NT)) * SCALE + hidden

    def softmax_of(scores):
        top = jnp.max(scores, axis=0, keepdims=True)
        expo = jnp.exp(scores - top)
        return expo, 1.0 / jnp.sum(expo, axis=0, keepdims=True)

    def context_of(block, expo, inverse):
        context = (mul(flipped[:LATENT, window_of(block)], expo.astype(bf16)) * inverse).astype(bf16)
        delta = jnp.sum(
            context.astype(f32) * context_grad[:, both(block)].astype(f32), axis=0, keepdims=True
        )
        return context, delta

    def score_grad_of(block, expo, inverse, delta):
        probs = expo * inverse
        grad = mul(keys[window_of(block), :LATENT], context_grad[:, both(block)]) - delta
        return (probs * grad * SCALE).astype(bf16), probs.astype(bf16)

    def lat_grad_of(block, score_grad, low):
        window = window_of(block)
        lat_grad = mul(flipped[:, window], score_grad)
        total[window, :LATENT] += mul(score_grad, query_lat[:, both(block)], NT) + mul(
            low, context_grad[:, both(block)], NT
        )
        total[window, LATENT:] += mul(score_grad, turned_of(block))
        return lat_grad[:LATENT, :].astype(bf16), lat_grad[LATENT:, :]

    def finish(block, context, lat_grad, turned_grad):
        pieces = []
        for e in pair:
            at = slice(e * BLOCK, (e + 1) * BLOCK)
            contexts[e, :, lanes(block)] = context[:, at]
            lat_grads[e, :, lanes(block)] = lat_grad[:, at]
            back_ref[slot(block), :, e * VHEAD:(e + 1) * VHEAD] = mul(
                context[:, at], value_ref[e], TN
            ).astype(bf16)
            pieces.append(mul(lat_grad[:, at], key_ref[e], TN))
            pieces.append(jnp.transpose(turned_grad[:, at]))
        back_ref[slot(block), :, PAIR * VHEAD:] = jnp.concatenate(pieces, axis=1).astype(bf16)

    for upper_block in range(blocks - 1, 0, -4):
        duo = tuple(range(upper_block, upper_block - 4, -1))
        scores = [scores_of(block) for block in duo]
        soft = [softmax_of(score) for score in scores]
        done = [context_of(block, *soft[n]) for n, block in enumerate(duo)]
        score_grads = [
            score_grad_of(block, *soft[n], done[n][1]) for n, block in enumerate(duo)
        ]
        last = [lat_grad_of(block, *score_grads[n]) for n, block in enumerate(duo)]
        for n, block in enumerate(duo):
            finish(block, done[n][0], *last[n])

    for e in pair:
        kv_ref[e, :, :NOPE] = mul(lat_grads[e], nope[e]).astype(bf16)
        kv_ref[e, :, NOPE:] = mul(contexts[e], grads[e]).astype(bf16)

    n_z, n_y, _, rows = keep_ref.shape[:4]
    empty = jnp.zeros((rows, KEY_PAD - KEY), bf16)
    for dz in range(n_z):
        for dy in range(n_y):
            head = lax.rem(z_here + dz, n_z) * n_y + lax.rem(y_here + dy, n_y)
            for dx in range(n_x):
                x = lax.rem(x_here + dx, n_x)
                for ref, parity in ((keep_ref, core), (send_ref, 1 - core)):
                    start = pl.multiple_of((2 * x + parity) * BLOCK + head * rows, rows)
                    ref[dz, dy, dx, :, :KEY] = total[pl.ds(start, rows), :].astype(bf16)
                    ref[dz, dy, dx, :, KEY:] = empty


def attention(place, docs, queries, own, other, key_up, value_up, grads, n_z, n_y):
    n_x = own.shape[0]
    tokens = 2 * n_x * BLOCK
    whole = lambda shape: pl.BlockSpec(shape, lambda i, place, docs: (0,) * len(shape))
    weights = pl.BlockSpec((PAIR, LATENT, NOPE), lambda i, place, docs: (place[0] * n_x + place[1], 0, 0))
    rows_shape = (n_z, n_y, n_x, BLOCK // (n_z * n_y), KEY_PAD)
    out_shapes = [
        (2 * n_x, BLOCK, PAIR * (VHEAD + QUERY)),
        (PAIR, LATENT, NOPE + VHEAD),
        rows_shape,
        rows_shape,
    ]
    return pl.pallas_call(
        attention_kernel,
        grid_spec=pltpu.PrefetchScalarGridSpec(
            num_scalar_prefetch=2,
            grid=(1,),
            in_specs=[
                whole(queries.shape),
                whole(own.shape),
                whole(other.shape),
                weights,
                weights,
                whole(grads.shape),
            ],
            out_specs=[whole(shape) for shape in out_shapes],
            scratch_shapes=[
                pltpu.VMEM((tokens, KEY), bf16),
                pltpu.VMEM((KEY, tokens), bf16),
                pltpu.VMEM((tokens, KEY), f32),
                pltpu.VMEM((LATENT, PAIR * tokens), bf16),
                pltpu.VMEM((LATENT, PAIR * tokens), bf16),
                pltpu.VMEM((PAIR, LATENT, tokens), bf16),
                pltpu.VMEM((PAIR, LATENT, tokens), bf16),
            ],
        ),
        out_shape=[jax.ShapeDtypeStruct(shape, bf16) for shape in out_shapes],
        name="attention",
        compiler_params=pltpu.CompilerParams(
            dimension_semantics=("arbitrary",), vmem_limit_bytes=48 * MIB
        ),
        cost_estimate=pl.CostEstimate(
            flops=9_000_000_000, bytes_accessed=15_000_000, transcendentals=1_600_000
        ),
    )(place, docs, queries, own, other, key_up, value_up, grads)


def join(back):
    slots, rows, width = back.shape
    value = PAIR * VHEAD

    def kernel(back_ref, attended_ref, query_grad_ref):
        for n in range(slots):
            attended_ref[:, n * value:(n + 1) * value] = back_ref[n, :, :value]
            at = slice(n * (width - value), (n + 1) * (width - value))
            query_grad_ref[:, at] = back_ref[n, :, value:]

    return pl.pallas_call(
        kernel,
        out_shape=[
            jax.ShapeDtypeStruct((rows, slots * value), bf16),
            jax.ShapeDtypeStruct((rows, slots * (width - value)), bf16),
        ],
        name="join",
    )(back)


def unfold(place, heads, pieces, begun):
    shape = jax.ShapeDtypeStruct((heads, LATENT, NOPE), f32)
    parts = [part for _, *parts in pieces for part in parts]
    operands = parts + [swapped(part) for part in parts]
    sides = parts[0].shape[0]
    n_x = heads // (2 * sides)
    count = 2 * len(pieces) * sides

    def kernel(place, *refs):
        sources = list(refs[:len(operands)])
        key_out, value_out, keys, values, sems = refs[-5:]
        started = []
        for n in range(2 * len(pieces)):
            x_away, *part = pieces[n % len(pieces)]
            core = place[0] if n < len(pieces) else 1 - place[0]
            x = lax.rem(place[1] + x_away, n_x)
            part = [sources.pop(0) for _ in part]
            for side in range(sides):
                slot = n * sides + side
                start = 0
                for ref in part:
                    rows = slice(start, start + ref.shape[1])
                    keys[slot, rows, :] = ref[side, :, :NOPE].astype(f32)
                    values[slot, rows, :] = ref[side, :, NOPE:].astype(f32)
                    start += ref.shape[1]
                head = core * (heads // 2) + x * sides + side
                for which, (done, out) in enumerate(((keys, key_out), (values, value_out))):
                    copy = pltpu.make_async_copy(done.at[slot], out.at[head], sems.at[which, slot])
                    copy.start()
                    started.append(copy)
        for copy in started:
            copy.wait()

    first = 1 + len(operands)
    return pl.pallas_call(
        kernel,
        grid_spec=pltpu.PrefetchScalarGridSpec(
            num_scalar_prefetch=1,
            grid=(1,),
            in_specs=[pl.BlockSpec(part.shape, lambda i, place: (0, 0, 0)) for part in operands]
            + [pl.BlockSpec(memory_space=pl.ANY)] * len(begun),
            out_specs=[pl.BlockSpec(memory_space=pl.ANY)] * 2,
            scratch_shapes=[pltpu.VMEM((count, LATENT, NOPE), f32)] * 2
            + [pltpu.SemaphoreType.DMA((2, count))],
        ),
        out_shape=[shape, shape],
        input_output_aliases={first: 0, first + 1: 1} if begun else {},
        name="unfold",
        compiler_params=pltpu.CompilerParams(vmem_limit_bytes=24 * MIB),
        cost_estimate=pl.CostEstimate(flops=0, bytes_accessed=4_000_000, transcendentals=0),
    )(place, *operands, *begun)


def pack(queries, n_head, n_x):
    rows, lanes = queries.shape
    lanes //= 2 * n_head * n_x

    def kernel(query_ref, out_ref):
        for head in range(n_head):
            for core in range(2):
                for x in range(n_x):
                    at = ((head * 2 + core) * n_x + x) * lanes
                    out_ref[(x * 2 + core) * n_head + head] = query_ref[:, at:at + lanes]

    return pl.pallas_call(
        kernel,
        out_shape=jax.ShapeDtypeStruct((2 * n_head * n_x, rows, lanes), bf16),
        name="pack",
    )(queries)


def swapped(value):
    return lax.ppermute(value, "core", [(0, 1), (1, 0)])


def shifted(value, axis, steps):
    count = lax.axis_size(axis)
    return lax.ppermute(value, axis, [(i, (i + steps) % count) for i in range(count)])


def exchanged(value, axes):
    return lax.all_to_all(value, axes, 0, 0, tiled=True)


def copies(value, count):
    return jnp.broadcast_to(value[None], (count,) + value.shape)


def added(*terms):
    return sum(term.astype(f32) for term in terms)


def folded(rows, axis):
    count = rows.shape[0]
    return added(rows[0], *[shifted(rows[s], axis, s) for s in range(1, count)])


def on_device(queries, latent, key_up, value_up, out_grad, block_docs):
    n_head = lax.axis_size(HEAD_AXES)
    n_x = lax.axis_size("x")
    core = lax.axis_index("core")
    x_here = lax.axis_index("x")
    n_z, n_y = [lax.axis_size(axis) for axis in HEAD_AXES]
    place = jnp.stack(
        [core, x_here] + [lax.axis_index(axis) for axis in HEAD_AXES]
    ).astype(jnp.int32)

    heads = key_up.shape[0]
    fine_axes = ("core", "x")
    grads = jnp.swapaxes(out_grad.reshape(BLOCK, 2 * n_x, -1), 0, 1)
    arrived = pack(queries, n_head, n_x)
    own = jnp.stack([latent] + [shifted(latent, "z", s) for s in range(1, n_z)])
    own, grads = lax.optimization_barrier((own, grads))
    grads = exchanged(grads, fine_axes)
    own = jnp.stack([own] + [shifted(own, "y", s) for s in range(1, n_y)]).reshape(BLOCK, KEY)
    own, arrived = lax.optimization_barrier((own, arrived))
    grads, arrived = lax.optimization_barrier((grads, arrived))
    arrived = exchanged(arrived, ("x", "core") + HEAD_AXES).reshape(2 * n_x * BLOCK, -1)
    own = jnp.stack([own] + [shifted(own, "x", s) for s in range(1, n_x)])
    other = swapped(own)

    back, kv, rows_keep, rows_send = attention(
        place, block_docs, arrived, own, other, key_up, value_up, grads, n_z, n_y
    )
    after = lax.optimization_barrier
    rows = added(rows_keep, swapped(rows_send)).astype(bf16)
    back = exchanged(back, fine_axes)
    kv = added(kv, shifted(kv, "dp", 1)).astype(bf16)
    rows = folded(rows, HEAD_AXES[0]).astype(bf16)
    kv, back = after((kv, back))
    upper, lower = kv[:, :HALF], kv[:, HALF:]
    before = [shifted(upper, "x", 1), shifted(lower, "x", 1)]
    behind = [shifted(lower, "x", -1), shifted(upper, "x", -1)]
    rows = folded(rows, HEAD_AXES[1]).astype(bf16)
    grads = unfold(place, heads, [(0, kv)], [])
    attended, query_grad = join(back)
    before[0], behind[0], rows, grads, attended, query_grad = after(
        (before[0], behind[0], rows, grads, attended, query_grad)
    )
    far = shifted(before[0], "x", 1), shifted(behind[0], "x", -1)
    rows = [rows[0]] + [shifted(rows[s], "x", s) for s in range(1, n_x)]
    grads = unfold(place, heads, [(n_x - 1, *before), (1, *behind[::-1])], grads)
    far, rows, grads, attended, query_grad = after((far, rows, grads, attended, query_grad))
    grads = unfold(place, heads, [(2,) + tuple(far)], grads)
    latent_grad = added(*rows)[:, :KEY]
    key_up_grad, value_up_grad = grads
    return (attended, query_grad, latent_grad, key_up_grad, value_up_grad)


def solution(mesh):
    n_dp, n_head, n_blk = mesh.devices.shape
    fine = Mesh(
        mesh.devices.reshape(n_dp, n_head // 2, 2, n_blk // 2, 2), ("dp", "z", "y", "x", "core")
    )
    head, blk = HEAD_AXES, ("x", "core")
    return jax.shard_map(
        on_device,
        mesh=fine,
        in_specs=(
            P(("dp",) + blk + head, None),
            P(("dp",) + blk + head, None),
            P(head, None, None),
            P(head, None, None),
            P(("dp",) + blk, head),
            P("dp", None),
        ),
        out_specs=(
            P(("dp",) + blk, head),
            P(("dp",) + blk, head),
            P(("dp",) + blk + head, None),
            P(head, None, None),
            P(head, None, None),
        ),
        check_vma=False,
    )
```

```python
import jax
import jax.numpy as jnp
from jax import lax
from jax.experimental import pallas as pl
from jax.experimental.pallas import tpu as pltpu
from jax.sharding import Mesh
from jax.sharding import PartitionSpec as P

NOPE = 128
ROPE = 64
LATENT = 512
VHEAD = 128
BLOCK = 128
QUERY = NOPE + ROPE
KEY = LATENT + ROPE
KEY_PAD = 640
HALF = LATENT // 2
DOC_MOST = 6
WINDOW = DOC_MOST * BLOCK
PAIR = 2
SCALE = QUERY ** -0.5
MIB = 1024 * 1024

bf16 = jnp.bfloat16
f32 = jnp.float32
NT = ((1,), (1,))
TN = ((0,), (0,))
HEAD_AXES = ("z", "y")


def mul(a, b, dims=((1,), (0,))):
    return lax.dot_general(a, b, (dims, ((), ())), preferred_element_type=f32)


def at_block(block):
    return pl.ds(pl.multiple_of(block * BLOCK, BLOCK), BLOCK)


def attention_kernel(
    place, docs, query_ref, own_ref, other_ref, key_ref, value_ref, grad_ref,
    back_ref, kv_ref, keep_ref, send_ref,
    keys, flipped, total, query_lat, context_grad, contexts, lat_grads,
):
    core, x_here, z_here, y_here = place[0], place[1], place[2], place[3]
    n_x = own_ref.shape[0]
    blocks = 2 * n_x
    pair = range(PAIR)
    doc_first = [
        sum([(docs[0, earlier] < docs[0, block]).astype(jnp.int32) for earlier in range(block)], 0)
        for block in range(blocks)
    ]
    for s in range(n_x):
        x = lax.rem(x_here + n_x - s, n_x)
        n_z, n_y, _, rows = keep_ref.shape[:4]
        for dz in range(n_z):
            for dy in range(n_y):
                head = lax.rem(z_here + n_z - dz, n_z) * n_y + lax.rem(y_here + n_y - dy, n_y)
                at_row = (dy * n_z + dz) * rows
                for ref, parity in ((own_ref, core), (other_ref, 1 - core)):
                    start = pl.multiple_of((2 * x + parity) * BLOCK + head * rows, rows)
                    keys[pl.ds(start, rows), :] = ref[s, at_row:at_row + rows, :]
    flipped[:LATENT, :] = jnp.transpose(keys[:, :LATENT])
    flipped[LATENT:, :] = jnp.transpose(keys[:, LATENT:])
    total[...] = jnp.zeros_like(total)

    slot = lambda block: (block % 2) * n_x + block // 2
    lanes = lambda block: slice(block * BLOCK, (block + 1) * BLOCK)
    columns = lambda block, e: slice((PAIR * block + e) * BLOCK, (PAIR * block + e + 1) * BLOCK)
    both = lambda block: slice(PAIR * block * BLOCK, PAIR * (block + 1) * BLOCK)
    nope = [query_ref[:, e * QUERY:e * QUERY + NOPE] for e in pair]
    grads = [
        jnp.concatenate(
            [grad_ref[slot(block), :, e * VHEAD:(e + 1) * VHEAD] for block in range(blocks)], axis=0
        )
        for e in pair
    ]
    for e in pair:
        spread_query = mul(key_ref[e], nope[e], NT).astype(bf16)
        spread_grad = mul(value_ref[e], grads[e], NT).astype(bf16)
        for block in range(blocks):
            query_lat[:, columns(block, e)] = spread_query[:, lanes(block)]
            context_grad[:, columns(block, e)] = spread_grad[:, lanes(block)]

    def window_of(block):
        return slice(max(block + 1 - DOC_MOST, 0) * BLOCK, (block + 1) * BLOCK)

    def turned_of(block):
        return jnp.concatenate(
            [query_ref[lanes(block), e * QUERY + NOPE:(e + 1) * QUERY] for e in pair], axis=0
        )

    def scores_of(block):
        window = window_of(block)
        shape = (window.stop - window.start, BLOCK)
        key_at = window.start + lax.broadcasted_iota(jnp.int32, shape, 0)
        query_at = block * BLOCK + lax.broadcasted_iota(jnp.int32, shape, 1)
        seen = (key_at >= doc_first[block] * BLOCK) & (key_at <= query_at)
        hidden = jnp.concatenate([jnp.where(seen, f32(0.0), f32(-1e30))] * PAIR, axis=1)
        near = mul(keys[window, :LATENT], query_lat[:, both(block)])
        return (near + mul(keys[window, LATENT:], turned_of(block), NT)) * SCALE + hidden

    def softmax_of(scores):
        top = jnp.max(scores, axis=0, keepdims=True)
        expo = jnp.exp(scores - top)
        return expo, 1.0 / jnp.sum(expo, axis=0, keepdims=True)

    def context_of(block, expo, inverse):
        context = (mul(flipped[:LATENT, window_of(block)], expo.astype(bf16)) * inverse).astype(bf16)
        delta = jnp.sum(
            context.astype(f32) * context_grad[:, both(block)].astype(f32), axis=0, keepdims=True
        )
        return context, delta

    def score_grad_of(block, expo, inverse, delta):
        probs = expo * inverse
        grad = mul(keys[window_of(block), :LATENT], context_grad[:, both(block)]) - delta
        return (probs * grad * SCALE).astype(bf16), probs.astype(bf16)

    def lat_grad_of(block, score_grad, low):
        window = window_of(block)
        lat_grad = mul(flipped[:, window], score_grad)
        total[window, :LATENT] += mul(score_grad, query_lat[:, both(block)], NT) + mul(
            low, context_grad[:, both(block)], NT
        )
        total[window, LATENT:] += mul(score_grad, turned_of(block))
        return lat_grad[:LATENT, :].astype(bf16), lat_grad[LATENT:, :]

    def finish(block, context, lat_grad, turned_grad):
        pieces = []
        for e in pair:
            at = slice(e * BLOCK, (e + 1) * BLOCK)
            contexts[e, :, lanes(block)] = context[:, at]
            lat_grads[e, :, lanes(block)] = lat_grad[:, at]
            back_ref[slot(block), :, e * VHEAD:(e + 1) * VHEAD] = mul(
                context[:, at], value_ref[e], TN
            ).astype(bf16)
            pieces.append(mul(lat_grad[:, at], key_ref[e], TN))
            pieces.append(jnp.transpose(turned_grad[:, at]))
        back_ref[slot(block), :, PAIR * VHEAD:] = jnp.concatenate(pieces, axis=1).astype(bf16)

    for upper_block in range(blocks - 1, 0, -8):
        duo = tuple(range(upper_block, upper_block - 8, -1))
        scores = [scores_of(block) for block in duo]
        soft = [softmax_of(score) for score in scores]
        done = [context_of(block, *soft[n]) for n, block in enumerate(duo)]
        score_grads = [
            score_grad_of(block, *soft[n], done[n][1]) for n, block in enumerate(duo)
        ]
        last = [lat_grad_of(block, *score_grads[n]) for n, block in enumerate(duo)]
        for n, block in enumerate(duo):
            finish(block, done[n][0], *last[n])

    for e in pair:
        kv_ref[e, :, :NOPE] = mul(lat_grads[e], nope[e]).astype(bf16)
        kv_ref[e, :, NOPE:] = mul(contexts[e], grads[e]).astype(bf16)

    n_z, n_y, _, rows = keep_ref.shape[:4]
    empty = jnp.zeros((rows, KEY_PAD - KEY), bf16)
    for dz in range(n_z):
        for dy in range(n_y):
            head = lax.rem(z_here + dz, n_z) * n_y + lax.rem(y_here + dy, n_y)
            for dx in range(n_x):
                x = lax.rem(x_here + dx, n_x)
                for ref, parity in ((keep_ref, core), (send_ref, 1 - core)):
                    start = pl.multiple_of((2 * x + parity) * BLOCK + head * rows, rows)
                    ref[dz, dy, dx, :, :KEY] = total[pl.ds(start, rows), :].astype(bf16)
                    ref[dz, dy, dx, :, KEY:] = empty


def attention(place, docs, queries, own, other, key_up, value_up, grads, n_z, n_y):
    n_x = own.shape[0]
    tokens = 2 * n_x * BLOCK
    whole = lambda shape: pl.BlockSpec(shape, lambda i, place, docs: (0,) * len(shape))
    weights = pl.BlockSpec((PAIR, LATENT, NOPE), lambda i, place, docs: (place[0] * n_x + place[1], 0, 0))
    rows_shape = (n_z, n_y, n_x, BLOCK // (n_z * n_y), KEY_PAD)
    out_shapes = [
        (2 * n_x, BLOCK, PAIR * (VHEAD + QUERY)),
        (PAIR, LATENT, NOPE + VHEAD),
        rows_shape,
        rows_shape,
    ]
    return pl.pallas_call(
        attention_kernel,
        grid_spec=pltpu.PrefetchScalarGridSpec(
            num_scalar_prefetch=2,
            grid=(1,),
            in_specs=[
                whole(queries.shape),
                whole(own.shape),
                whole(other.shape),
                weights,
                weights,
                whole(grads.shape),
            ],
            out_specs=[whole(shape) for shape in out_shapes],
            scratch_shapes=[
                pltpu.VMEM((tokens, KEY), bf16),
                pltpu.VMEM((KEY, tokens), bf16),
                pltpu.VMEM((tokens, KEY), f32),
                pltpu.VMEM((LATENT, PAIR * tokens), bf16),
                pltpu.VMEM((LATENT, PAIR * tokens), bf16),
                pltpu.VMEM((PAIR, LATENT, tokens), bf16),
                pltpu.VMEM((PAIR, LATENT, tokens), bf16),
            ],
        ),
        out_shape=[jax.ShapeDtypeStruct(shape, bf16) for shape in out_shapes],
        name="attention",
        compiler_params=pltpu.CompilerParams(
            dimension_semantics=("arbitrary",), vmem_limit_bytes=48 * MIB
        ),
        cost_estimate=pl.CostEstimate(
            flops=9_000_000_000, bytes_accessed=15_000_000, transcendentals=1_600_000
        ),
    )(place, docs, queries, own, other, key_up, value_up, grads)


def join(back):
    slots, rows, width = back.shape
    value = PAIR * VHEAD

    def kernel(back_ref, attended_ref, query_grad_ref):
        for n in range(slots):
            attended_ref[:, n * value:(n + 1) * value] = back_ref[n, :, :value]
            at = slice(n * (width - value), (n + 1) * (width - value))
            query_grad_ref[:, at] = back_ref[n, :, value:]

    return pl.pallas_call(
        kernel,
        out_shape=[
            jax.ShapeDtypeStruct((rows, slots * value), bf16),
            jax.ShapeDtypeStruct((rows, slots * (width - value)), bf16),
        ],
        name="join",
    )(back)


def unfold(place, heads, pieces, begun):
    shape = jax.ShapeDtypeStruct((heads, LATENT, NOPE), f32)
    parts = [part for _, *parts in pieces for part in parts]
    operands = parts + [swapped(part) for part in parts]
    sides = parts[0].shape[0]
    n_x = heads // (2 * sides)
    count = 2 * len(pieces) * sides

    def kernel(place, *refs):
        sources = list(refs[:len(operands)])
        key_out, value_out, keys, values, sems = refs[-5:]
        started = []
        for n in range(2 * len(pieces)):
            x_away, *part = pieces[n % len(pieces)]
            core = place[0] if n < len(pieces) else 1 - place[0]
            x = lax.rem(place[1] + x_away, n_x)
            part = [sources.pop(0) for _ in part]
            for side in range(sides):
                slot = n * sides + side
                start = 0
                for ref in part:
                    rows = slice(start, start + ref.shape[1])
                    keys[slot, rows, :] = ref[side, :, :NOPE].astype(f32)
                    values[slot, rows, :] = ref[side, :, NOPE:].astype(f32)
                    start += ref.shape[1]
                head = core * (heads // 2) + x * sides + side
                for which, (done, out) in enumerate(((keys, key_out), (values, value_out))):
                    copy = pltpu.make_async_copy(done.at[slot], out.at[head], sems.at[which, slot])
                    copy.start()
                    started.append(copy)
        for copy in started:
            copy.wait()

    first = 1 + len(operands)
    return pl.pallas_call(
        kernel,
        grid_spec=pltpu.PrefetchScalarGridSpec(
            num_scalar_prefetch=1,
            grid=(1,),
            in_specs=[pl.BlockSpec(part.shape, lambda i, place: (0, 0, 0)) for part in operands]
            + [pl.BlockSpec(memory_space=pl.ANY)] * len(begun),
            out_specs=[pl.BlockSpec(memory_space=pl.ANY)] * 2,
            scratch_shapes=[pltpu.VMEM((count, LATENT, NOPE), f32)] * 2
            + [pltpu.SemaphoreType.DMA((2, count))],
        ),
        out_shape=[shape, shape],
        input_output_aliases={first: 0, first + 1: 1} if begun else {},
        name="unfold",
        compiler_params=pltpu.CompilerParams(vmem_limit_bytes=24 * MIB),
        cost_estimate=pl.CostEstimate(flops=0, bytes_accessed=4_000_000, transcendentals=0),
    )(place, *operands, *begun)


def pack(queries, n_head, n_x):
    rows, lanes = queries.shape
    lanes //= 2 * n_head * n_x

    def kernel(query_ref, out_ref):
        for head in range(n_head):
            for core in range(2):
                for x in range(n_x):
                    at = ((head * 2 + core) * n_x + x) * lanes
                    out_ref[(x * 2 + core) * n_head + head] = query_ref[:, at:at + lanes]

    return pl.pallas_call(
        kernel,
        out_shape=jax.ShapeDtypeStruct((2 * n_head * n_x, rows, lanes), bf16),
        name="pack",
    )(queries)


def swapped(value):
    return lax.ppermute(value, "core", [(0, 1), (1, 0)])


def shifted(value, axis, steps):
    count = lax.axis_size(axis)
    return lax.ppermute(value, axis, [(i, (i + steps) % count) for i in range(count)])


def exchanged(value, axes):
    return lax.all_to_all(value, axes, 0, 0, tiled=True)


def copies(value, count):
    return jnp.broadcast_to(value[None], (count,) + value.shape)


def added(*terms):
    return sum(term.astype(f32) for term in terms)


def folded(rows, axis):
    count = rows.shape[0]
    return added(rows[0], *[shifted(rows[s], axis, s) for s in range(1, count)])


def on_device(queries, latent, key_up, value_up, out_grad, block_docs):
    n_head = lax.axis_size(HEAD_AXES)
    n_x = lax.axis_size("x")
    core = lax.axis_index("core")
    x_here = lax.axis_index("x")
    n_z, n_y = [lax.axis_size(axis) for axis in HEAD_AXES]
    place = jnp.stack(
        [core, x_here] + [lax.axis_index(axis) for axis in HEAD_AXES]
    ).astype(jnp.int32)

    heads = key_up.shape[0]
    fine_axes = ("core", "x")
    grads = jnp.swapaxes(out_grad.reshape(BLOCK, 2 * n_x, -1), 0, 1)
    arrived = pack(queries, n_head, n_x)
    own = jnp.stack([latent] + [shifted(latent, "z", s) for s in range(1, n_z)])
    own, grads = lax.optimization_barrier((own, grads))
    grads = exchanged(grads, fine_axes)
    own = jnp.stack([own] + [shifted(own, "y", s) for s in range(1, n_y)]).reshape(BLOCK, KEY)
    own, arrived = lax.optimization_barrier((own, arrived))
    grads, arrived = lax.optimization_barrier((grads, arrived))
    arrived = exchanged(arrived, ("x", "core") + HEAD_AXES).reshape(2 * n_x * BLOCK, -1)
    own = jnp.stack([own] + [shifted(own, "x", s) for s in range(1, n_x)])
    other = swapped(own)

    back, kv, rows_keep, rows_send = attention(
        place, block_docs, arrived, own, other, key_up, value_up, grads, n_z, n_y
    )
    after = lax.optimization_barrier
    rows = added(rows_keep, swapped(rows_send)).astype(bf16)
    back = exchanged(back, fine_axes)
    kv = added(kv, shifted(kv, "dp", 1)).astype(bf16)
    rows = folded(rows, HEAD_AXES[0]).astype(bf16)
    kv, back = after((kv, back))
    upper, lower = kv[:, :HALF], kv[:, HALF:]
    before = [shifted(upper, "x", 1), shifted(lower, "x", 1)]
    behind = [shifted(lower, "x", -1), shifted(upper, "x", -1)]
    rows = folded(rows, HEAD_AXES[1]).astype(bf16)
    grads = unfold(place, heads, [(0, kv)], [])
    attended, query_grad = join(back)
    before[0], behind[0], rows, grads, attended, query_grad = after(
        (before[0], behind[0], rows, grads, attended, query_grad)
    )
    far = shifted(before[0], "x", 1), shifted(behind[0], "x", -1)
    rows = [rows[0]] + [shifted(rows[s], "x", s) for s in range(1, n_x)]
    grads = unfold(place, heads, [(n_x - 1, *before), (1, *behind[::-1])], grads)
    far, rows, grads, attended, query_grad = after((far, rows, grads, attended, query_grad))
    grads = unfold(place, heads, [(2,) + tuple(far)], grads)
    latent_grad = added(*rows)[:, :KEY]
    key_up_grad, value_up_grad = grads
    return (attended, query_grad, latent_grad, key_up_grad, value_up_grad)


def solution(mesh):
    n_dp, n_head, n_blk = mesh.devices.shape
    fine = Mesh(
        mesh.devices.reshape(n_dp, n_head // 2, 2, n_blk // 2, 2), ("dp", "z", "y", "x", "core")
    )
    head, blk = HEAD_AXES, ("x", "core")
    return jax.shard_map(
        on_device,
        mesh=fine,
        in_specs=(
            P(("dp",) + blk + head, None),
            P(("dp",) + blk + head, None),
            P(head, None, None),
            P(head, None, None),
            P(("dp",) + blk, head),
            P("dp", None),
        ),
        out_specs=(
            P(("dp",) + blk, head),
            P(("dp",) + blk, head),
            P(("dp",) + blk + head, None),
            P(head, None, None),
            P(head, None, None),
        ),
        check_vma=False,
    )
```
